256 devices in a mesh: seq: 128 (over x_lo, y, z, core), ch: 2 (over x_hi).
Axes of the slice: x: 4 (x_hi: 2, x_lo: 2; x = x_hi * 2 + x_lo), y: 4, z: 8, core: 2. Of those that a mesh axis runs over, the one named last changes fastest.
Arguments:
- tokens: bfloat16 [131072, 1536], P('seq', 'ch'), may hold values from -16 to 16
- spectrum: bfloat16 [2, 512, 256, 768], P(None, 'seq', None, 'ch'), may hold values from -4 to 4
- skip: float32 [1536], P('ch'), may hold values from -1 to 1
- gain: float32 [1536], P('ch'), may hold values from 0.1 to 1.9
- mix_in: bfloat16 [4, 384, 384], P('ch'), may hold values from -0.3125 to 0.3125
- w_up: bfloat16 [4, 384, 1536], P('ch'), may hold values from -0.3125 to 0.3125
- w_down: bfloat16 [4, 1536, 384], P('ch'), may hold values from -0.15625 to 0.15625
- mix_out: bfloat16 [4, 384, 384], P('ch'), may hold values from -0.3125 to 0.3125
Outputs:
- layer_out: bfloat16 [131072, 1536], P('seq', 'ch')
The draws below stay inside these ranges and needn't reach their ends.
All inputs are finite; a program needn't handle non-finite values.
Results may differ from the reference program's by a relative error of at most 0.012.
Values may be sent and summed in bfloat16 or wider, within the bound.
No kernel may reach another device: no remote copies, remote signals or barrier semaphores. Data moves between devices by JAX's collectives and lax.ppermute only.
A program may use at most 128 MiB of HBM per device.

```python
import math
import jax
import jax.numpy as jnp
from jax import lax

D = 1536
FF = 6144
NB = 4
PBLK = 256
QBLK = 512
SEQ_LEN = 131072


def draw_tokens(key, part):
    key = jax.random.fold_in(key, 17)
    subkeys = jax.random.split(key, 4)
    columns = 0.4 * 3.0 ** (jnp.arange(D, dtype=jnp.float32) / (D - 1))
    columns = columns * jnp.exp(jax.random.uniform(subkeys[1], (1, D), minval=-0.35, maxval=0.35))
    ramp = 0.8 * (1.0 - jnp.arange(D, dtype=jnp.float32) / (D - 1))
    common = jnp.clip(jax.random.normal(subkeys[3], (SEQ_LEN, 1)), -2.0, 2.0)
    scales = jnp.exp(jax.random.uniform(subkeys[0], (SEQ_LEN, 1), minval=math.log(0.45), maxval=math.log(2.2)))
    values = jnp.clip(jax.random.normal(subkeys[2], (SEQ_LEN, D)), -2.5, 2.5) + ramp * common
    return (values * scales * columns).astype(jnp.bfloat16)


def levels(own_key, shape, cuts, low, high):
    level, own = 1.0, jax.random.fold_in(own_key, 6)
    for dim, parts in cuts:
        steps = jnp.exp(jax.random.uniform(jax.random.fold_in(own, dim), (parts,), jnp.float32, low / len(cuts), high / len(cuts)))
        level = level * jnp.repeat(steps, shape[dim] // parts).reshape([-1 if axis == dim else 1 for axis in range(len(shape))])
    return level


def normal_values(key, extent, deviation, reach, cuts=(), kind=jnp.bfloat16):
    level = levels(key, extent, cuts, -0.22, 0.18) if cuts else 1.0
    values = jax.random.normal(key, extent, jnp.float32) * deviation * level
    return jnp.minimum(jnp.maximum(values, -reach), reach).astype(kind)


def setup_inputs(seed: int = 0) -> dict:
    splits = jax.random.split(jax.random.key(seed), 9)
    tokens = draw_tokens(jax.random.fold_in(splits[8], 71), 0)
    spectrum = normal_values(splits[1], (2, QBLK, PBLK, D // 2), 0.7, 4.0, ((1, 128), (3, 2)))
    skip = jnp.clip(jax.random.uniform(splits[2], (D,), jnp.float32, -1.0, 1.0) * levels(splits[2], (D,), ((0, 2),), -0.4, 0.0), -1.0, 1.0)
    gain = jnp.clip(1.0 + 0.18 * jax.random.normal(splits[3], (D,), jnp.float32), 0.1, 1.9)
    mix_in = normal_values(splits[4], (NB, D // NB, D // NB), (D // NB) ** -0.5, 0.3125, ((0, 2),))
    w_up = normal_values(splits[5], (NB, D // NB, FF // NB), (D // NB) ** -0.5, 0.3125, ((0, 2),))
    w_down = normal_values(splits[6], (NB, FF // NB, D // NB), (FF // NB) ** -0.5, 0.15625, ((0, 2),))
    mix_out = normal_values(splits[7], (NB, D // NB, D // NB), (D // NB) ** -0.5, 0.3125, ((0, 2),))
    return {"tokens": tokens, "spectrum": spectrum, "skip": skip, "gain": gain, "mix_in": mix_in, "w_up": w_up, "w_down": w_down, "mix_out": mix_out}


def dft_table(length):
    index = jnp.arange(length, dtype=jnp.int32)
    prod_index = index[:, None] * index[None, :] % length
    angle = prod_index.astype(jnp.float32) * (2.0 * math.pi / length)
    return (jnp.cos(angle).astype(jnp.bfloat16), jnp.sin(angle).astype(jnp.bfloat16))

def turn_table(first_index, second_index, length):
    prod_index = first_index[:, None] * second_index[None, :] % length
    angle = prod_index.astype(jnp.float32) * (2.0 * math.pi / length)
    return (jnp.cos(angle), jnp.sin(angle))

def product(form, left, right):
    return jnp.einsum(form, left.astype(jnp.float32), right.astype(jnp.float32), precision=lax.Precision.HIGHEST)

def long_conv(block, kernel):
    cos_long, sin_long = dft_table(QBLK)
    cos_short, sin_short = dft_table(PBLK)
    turn_cos, turn_sin = turn_table(jnp.arange(QBLK, dtype=jnp.int32), jnp.arange(PBLK, dtype=jnp.int32), SEQ_LEN)
    turn_cos = turn_cos[:, :, None]
    turn_sin = turn_sin[:, :, None]
    kernel = jnp.repeat(kernel, 2, axis=3)
    first_real = product('qtc,qk->ktc', block, cos_long)
    first_imag = -product('qtc,qk->ktc', block, sin_long)
    turned_real = (first_real * turn_cos + first_imag * turn_sin).astype(jnp.bfloat16)
    turned_imag = (first_imag * turn_cos - first_real * turn_sin).astype(jnp.bfloat16)
    spectral_real = product('ktc,tm->kmc', turned_real, cos_short) + product('ktc,tm->kmc', turned_imag, sin_short)
    spectral_imag = product('ktc,tm->kmc', turned_imag, cos_short) - product('ktc,tm->kmc', turned_real, sin_short)
    kernel_real = kernel[0].astype(jnp.float32)
    kernel_imag = kernel[1].astype(jnp.float32)
    filtered_real = (spectral_real * kernel_real - spectral_imag * kernel_imag).astype(jnp.bfloat16)
    filtered_imag = (spectral_real * kernel_imag + spectral_imag * kernel_real).astype(jnp.bfloat16)
    back_real = product('kmc,mt->ktc', filtered_real, cos_short) - product('kmc,mt->ktc', filtered_imag, sin_short)
    back_imag = product('kmc,mt->ktc', filtered_real, sin_short) + product('kmc,mt->ktc', filtered_imag, cos_short)
    returned_real = (back_real * turn_cos - back_imag * turn_sin).astype(jnp.bfloat16)
    returned_imag = (back_real * turn_sin + back_imag * turn_cos).astype(jnp.bfloat16)
    result = product('ktc,kq->qtc', returned_real, cos_long) - product('ktc,kq->qtc', returned_imag, sin_long)
    return (result * (1.0 / SEQ_LEN)).astype(jnp.bfloat16)

def row_block(rows, conv_rows, skip, gain, mix_in, w_up, w_down, mix_out):
    count = rows.shape[0]
    inner = D // NB
    piece = inner // NB
    values = rows.astype(jnp.float32)
    mixed = conv_rows.astype(jnp.float32) + skip * values
    hidden = values + mixed * jax.nn.sigmoid(values)
    mean = lax.optimization_barrier(jnp.mean(hidden, axis=1, keepdims=True))
    centered = hidden - mean
    variance = lax.optimization_barrier(jnp.mean(centered * centered, axis=1, keepdims=True))
    normed = (centered * lax.rsqrt(variance + 1e-05) * gain).astype(jnp.bfloat16)
    first_mix = product('rbi,bij->rbj', normed.reshape(count, NB, inner), mix_in).astype(jnp.bfloat16)
    shuffled = first_mix.reshape(count, NB, NB, piece).transpose(0, 2, 1, 3).reshape(count, NB, inner)
    up = product('rci,cif->rcf', shuffled, w_up)
    activated = jax.nn.gelu(up, approximate=True).astype(jnp.bfloat16)
    down = product('rcf,cfi->rci', activated, w_down).astype(jnp.bfloat16)
    unshuffled = down.reshape(count, NB, NB, piece).transpose(0, 2, 1, 3).reshape(count, NB, inner)
    outcome = product('rbi,bij->rbj', unshuffled, mix_out).reshape(count, D)
    return (hidden + outcome).astype(jnp.bfloat16)

def reference(tokens, spectrum, skip, gain, mix_in, w_up, w_down, mix_out):
    width_block = 128 if D % 128 == 0 else D
    count_blocks = D // width_block
    half_block = width_block // 2
    grid = tokens.reshape(QBLK, PBLK, count_blocks, width_block).transpose(2, 0, 1, 3)
    kernels = spectrum.reshape(2, QBLK, PBLK, count_blocks, half_block).transpose(3, 0, 1, 2, 4)
    conv = lax.map(lambda pair: long_conv(pair[0], pair[1]), (grid, kernels))
    conv = conv.transpose(1, 2, 0, 3).reshape(SEQ_LEN, D)
    row_size = min(SEQ_LEN, 8192)
    row_count = SEQ_LEN // row_size
    token_rows = tokens.reshape(row_count, row_size, D)
    conv_rows = conv.reshape(row_count, row_size, D)
    result = lax.map(lambda pair: row_block(pair[0], pair[1], skip, gain, mix_in, w_up, w_down, mix_out), (token_rows, conv_rows))
    return result.reshape(SEQ_LEN, D)
```

```python
import functools
import math

import jax
import jax.numpy as jnp
import ml_dtypes
import numpy as np
from jax import lax
from jax.experimental import pallas as pl
from jax.experimental.pallas import tpu as pltpu
from jax.sharding import PartitionSpec as P

D = 1536
NB = 4
PBLK = 256
QBLK = 512
LANES = 128
F32 = jnp.float32
BF16 = jnp.bfloat16
VMEM_LIMIT = 56 * 1024 * 1024


def dft_numpy(length):
    index = np.arange(length, dtype=np.int64)
    angle = (index[:, None] * index[None, :] % length).astype(np.float32)
    angle = angle * np.float32(2.0 * math.pi / length)
    return (
        np.cos(angle).astype(ml_dtypes.bfloat16).astype(np.float32),
        np.sin(angle).astype(ml_dtypes.bfloat16).astype(np.float32),
    )


def make_tables(groups):
    low = QBLK // groups
    order = (np.arange(groups)[None, :] * low + np.arange(low)[:, None]).reshape(-1)
    cos_long, sin_long = dft_numpy(QBLK)
    cos_long, sin_long = cos_long[order][:, order], sin_long[order][:, order]
    cos_short, sin_short = dft_numpy(PBLK)
    forward = np.concatenate([cos_long, -sin_long], axis=0)
    backward = np.concatenate([cos_long, -sin_long], axis=1) * np.float32(1.0 / (PBLK * QBLK))
    second = np.block([[cos_short, -sin_short], [sin_short, cos_short]])
    third = np.block([[cos_short, sin_short], [-sin_short, cos_short]])
    seq_len = PBLK * QBLK
    angle = (order[:, None].astype(np.int64) * np.arange(PBLK)[None, :] % seq_len).astype(np.float32)
    angle = angle * np.float32(2.0 * math.pi / seq_len)
    half = [t.astype(ml_dtypes.bfloat16) for t in (forward, second, third, backward)]
    return half + [np.cos(angle).astype(np.float32), np.sin(angle).astype(np.float32)]


def pair_split():
    table = np.zeros((2 * LANES, 2 * LANES), np.float32)
    for e in range(2):
        for d in range(LANES):
            table[e * LANES + d, 2 * d + e] = 1.0
    return table.astype(ml_dtypes.bfloat16)


def nt_dot(left, right):
    return lax.dot_general(left, right, (((1,), (1,)), ((), ())), preferred_element_type=F32)


def pack_kernel(tokens_ref, spectrum_ref, split_ref, out_ref, wide):
    split = split_ref[...]
    for block in range(8):
        low, half = block // 2, block % 2
        turned = nt_dot(split, tokens_ref[block * LANES : (block + 1) * LANES, :])
        for e in range(2):
            row = e * 8 + half * 4 + low
            wide[pl.ds(row, LANES, stride=32), :] = turned[e * LANES : (e + 1) * LANES]
    lane = lax.broadcasted_iota(jnp.int32, (LANES, LANES), 0)
    eye = (lane == lax.broadcasted_iota(jnp.int32, (LANES, LANES), 1)).astype(F32).astype(BF16)
    for part in range(2):
        for low in range(4):
            turned = nt_dot(eye, spectrum_ref[part, low])
            for half in range(2):
                row = 16 + part * 8 + half * 4 + low
                wide[pl.ds(row, LANES, stride=32), :] = turned[:, half * LANES : (half + 1) * LANES]
    out_ref[...] = wide[...].reshape(LANES, 32, LANES).astype(BF16)


def pack(tokens, spectrum):
    return pl.pallas_call(
        pack_kernel,
        grid=(3,),
        in_specs=[
            pl.BlockSpec((1024, 256), lambda i: (0, i)),
            pl.BlockSpec((2, 4, 256, LANES), lambda i: (0, 0, 0, i)),
            pl.BlockSpec((256, 256), lambda i: (0, 0)),
        ],
        out_specs=pl.BlockSpec((LANES, 32, LANES), lambda i: (0, i, 0)),
        out_shape=jax.ShapeDtypeStruct((LANES, 96, LANES), BF16),
        scratch_shapes=[pltpu.VMEM((LANES * 32, LANES), F32)],
        compiler_params=pltpu.CompilerParams(vmem_limit_bytes=VMEM_LIMIT),
        cost_estimate=pl.CostEstimate(flops=2 * 10**9, bytes_accessed=6 * 2**20, transcendentals=0),
        name="pack",
    )(tokens, spectrum, pair_split())


def conv_kernel(chunks, data_ref, forward_ref, second_ref, third_ref, backward_ref, cos_ref, sin_ref, *rest):
    out_refs, (wide, back), outs = rest[:chunks], rest[chunks : chunks + 2], rest[chunks + 2 :]
    slot = pl.program_id(0)
    rows_each = 48 // chunks
    low_each = 4 // chunks
    wide[...] = data_ref[...].reshape(LANES * 32, LANES).astype(F32)

    def piece(row):
        return wide[pl.ds(row, LANES, stride=32), :]

    def filters(part):
        return jnp.concatenate(
            [
                jnp.concatenate([piece(16 + part * 8 + half * 4 + low) for half in range(2)], axis=1)
                for low in range(4)
            ],
            axis=0,
        )

    filter_real, filter_imag = filters(0), filters(1)
    for e in range(2):
        block = jnp.concatenate(
            [
                jnp.concatenate([piece(e * 8 + half * 4 + low) for half in range(2)], axis=1).astype(BF16)
                for low in range(4)
            ],
            axis=0,
        )
        first = jnp.dot(forward_ref[...], block, preferred_element_type=F32)
        first_real, first_imag = first[:QBLK], first[QBLK:]
        turn_cos, turn_sin = cos_ref[...], sin_ref[...]
        turned = jnp.concatenate(
            [
                (first_real * turn_cos + first_imag * turn_sin).astype(BF16),
                (first_imag * turn_cos - first_real * turn_sin).astype(BF16),
            ],
            axis=1,
        )
        spectral = jnp.dot(turned, second_ref[...], preferred_element_type=F32)
        spectral_real, spectral_imag = spectral[:, :PBLK], spectral[:, PBLK:]
        filtered = jnp.concatenate(
            [
                (spectral_real * filter_real - spectral_imag * filter_imag).astype(BF16),
                (spectral_real * filter_imag + spectral_imag * filter_real).astype(BF16),
            ],
            axis=1,
        )
        third = jnp.dot(filtered, third_ref[...], preferred_element_type=F32)
        back_real, back_imag = third[:, :PBLK], third[:, PBLK:]
        back[:QBLK, :] = (back_real * turn_cos - back_imag * turn_sin).astype(BF16)
        back[QBLK:, :] = (back_real * turn_sin + back_imag * turn_cos).astype(BF16)
        conv = jnp.dot(backward_ref[...], back[...], preferred_element_type=F32)
        for low in range(4):
            for half in range(2):
                row = ((slot * 2 + e) * 2 + half) * low_each + low % low_each
                outs[low // low_each][pl.ds(row, LANES, stride=rows_each), :] = conv[
                    low * LANES : (low + 1) * LANES, half * LANES : (half + 1) * LANES
                ]

    @pl.when(slot == 2)
    def _():
        for q in range(chunks):
            out_refs[q][...] = outs[q][...].astype(BF16)


def convolve(data, tables, chunks):
    rows = LANES * 48 // chunks
    whole = lambda shape: pl.BlockSpec(shape, lambda i: (0,) * len(shape))
    return pl.pallas_call(
        functools.partial(conv_kernel, chunks),
        grid=(3,),
        in_specs=[pl.BlockSpec((LANES, 32, LANES), lambda i: (0, i, 0))] + [whole(t.shape) for t in tables],
        out_specs=[whole((rows, LANES))] * chunks,
        out_shape=[jax.ShapeDtypeStruct((rows, LANES), BF16)] * chunks,
        scratch_shapes=[
            pltpu.VMEM((LANES * 32, LANES), F32),
            pltpu.VMEM((2 * QBLK, PBLK), BF16),
        ]
        + [pltpu.VMEM((rows, LANES), F32)] * chunks,
        compiler_params=pltpu.CompilerParams(vmem_limit_bytes=VMEM_LIMIT),
        cost_estimate=pl.CostEstimate(flops=64 * 10**8, bytes_accessed=8 * 2**20, transcendentals=0),
        name="convolve",
    )(data, *tables)


def hidden_kernel(lows, conv_ref, tokens_ref, skip_ref, split_ref, hidden_ref, stats_ref, wide):
    per_slot = 4 * lows
    wide[...] = conv_ref[...].astype(F32)
    split = split_ref[...]
    lane = lax.broadcasted_iota(jnp.int32, (LANES, LANES), 1)
    for block in range(2 * lows):
        low, half = block // 2, block % 2
        rows = slice(block * LANES, (block + 1) * LANES)
        pieces = []
        for slot in range(3):
            turned = jnp.concatenate(
                [
                    wide[pl.ds(((slot * 2 + e) * 2 + half) * lows + low, LANES, stride=3 * per_slot), :].T
                    for e in range(2)
                ],
                axis=1,
            ).astype(BF16)
            conv = jnp.dot(turned, split, preferred_element_type=F32)
            cols = slice(slot * 256, (slot + 1) * 256)
            values = tokens_ref[rows, cols].astype(F32)
            mixed = conv + skip_ref[:, cols] * values
            pieces.append(values + mixed * jax.nn.sigmoid(values))
        hidden = jnp.concatenate(pieces, axis=1)
        hidden_ref[rows, :] = hidden
        mean = jnp.mean(hidden, axis=1, keepdims=True)
        centered = hidden - mean
        square = jnp.sum(centered * centered, axis=1, keepdims=True)
        both = jnp.where(lane == 0, mean, jnp.where(lane == 1, square, 0.0))
        stats_ref[block] = both.T[:8]


def make_hidden(conv, tokens, skip, chunk, chunks):
    rows = tokens.shape[0] // chunks
    return pl.pallas_call(
        functools.partial(hidden_kernel, 4 // chunks),
        grid=(1,),
        in_specs=[
            pl.BlockSpec(conv.shape, lambda i: (0, 0)),
            pl.BlockSpec((rows, 768), lambda i: (chunk, 0)),
            pl.BlockSpec((1, 768), lambda i: (0, 0)),
            pl.BlockSpec((256, 256), lambda i: (0, 0)),
        ],
        out_specs=[
            pl.BlockSpec((rows, 768), lambda i: (0, 0)),
            pl.BlockSpec((rows // LANES, 8, LANES), lambda i: (0, 0, 0)),
        ],
        out_shape=[
            jax.ShapeDtypeStruct((rows, 768), F32),
            jax.ShapeDtypeStruct((rows // LANES, 8, LANES), F32),
        ],
        scratch_shapes=[pltpu.VMEM(conv.shape, F32)],
        compiler_params=pltpu.CompilerParams(vmem_limit_bytes=VMEM_LIMIT),
        cost_estimate=pl.CostEstimate(flops=4 * 10**8, bytes_accessed=6 * 2**20 // chunks, transcendentals=10**6),
        name="hidden",
    )(conv, tokens, skip, pair_split())


def mix_kernel(hidden_ref, mine_ref, other_ref, gain_ref, weight_ref, own_ref, send_ref):
    width = hidden_ref.shape[1]
    for block in range(hidden_ref.shape[0] // LANES):
        rows = slice(block * LANES, (block + 1) * LANES)
        mine = jnp.concatenate([mine_ref[block]] * 16, axis=0).T
        other = jnp.concatenate([other_ref[block]] * 16, axis=0).T
        mean = 0.5 * (mine[:, 0:1] + other[:, 0:1])
        gap = mine[:, 0:1] - other[:, 0:1]
        square = mine[:, 1:2] + other[:, 1:2] + gap * gap * (0.5 * width)
        scale = lax.rsqrt(square / (2 * width) + 1e-05)
        normed = ((hidden_ref[rows, :] - mean) * scale * gain_ref[...]).astype(BF16)
        mixed = jnp.dot(normed, weight_ref[...], preferred_element_type=F32).astype(BF16)
        own_ref[rows, :] = mixed[:, : width // 2]
        send_ref[rows, :] = mixed[:, width // 2 :]


def first_mix(hidden, mine, other, gain, weight):
    rows, width = hidden.shape
    return pl.pallas_call(
        mix_kernel,
        out_shape=[jax.ShapeDtypeStruct((rows, width // 2), BF16)] * 2,
        compiler_params=pltpu.CompilerParams(vmem_limit_bytes=VMEM_LIMIT),
        cost_estimate=pl.CostEstimate(flops=2 * rows * 768 * 768, bytes_accessed=rows * 768 * 6, transcendentals=0),
        name="first_mix",
    )(hidden, mine, other, gain, weight)


def mlp_kernel(own_ref, rem_ref, up_own_ref, up_rem_ref, down_own_ref, down_send_ref, keep_ref, send_ref):
    rows = min(256, own_ref.shape[0])
    for block in range(own_ref.shape[0] // rows):
        at = slice(block * rows, (block + 1) * rows)
        keep, send = [], []
        for c in range(2):
            window = slice(c * LANES, c * LANES + 256)
            up = jnp.dot(own_ref[at, window], up_own_ref[c], preferred_element_type=F32)
            up = up + jnp.dot(rem_ref[at, window], up_rem_ref[c], preferred_element_type=F32)
            active = jax.nn.gelu(up, approximate=True).astype(BF16)
            keep.append(jnp.dot(active, down_own_ref[c], preferred_element_type=F32))
            send.append(jnp.dot(active, down_send_ref[c], preferred_element_type=F32))
        for parts, ref in ((keep, keep_ref), (send, send_ref)):
            ref[at, 0:128] = parts[0][:, 0:128].astype(BF16)
            ref[at, 128:256] = (parts[0][:, 128:256] + parts[1][:, 0:128]).astype(BF16)
            ref[at, 256:384] = parts[1][:, 128:256].astype(BF16)


def mlp(own, rem, up_own, up_rem, down_own, down_send):
    rows, width = own.shape
    return pl.pallas_call(
        mlp_kernel,
        out_shape=[jax.ShapeDtypeStruct((rows, width), BF16)] * 2,
        compiler_params=pltpu.CompilerParams(vmem_limit_bytes=VMEM_LIMIT),
        cost_estimate=pl.CostEstimate(
            flops=rows * 48 * 10**5, bytes_accessed=6 * 2**20 + rows * 3072, transcendentals=rows * 3072
        ),
        name="mlp",
    )(own, rem, up_own, up_rem, down_own, down_send)


def last_kernel(hidden_ref, keep_ref, rem_ref, weight_ref, out_ref):
    half = keep_ref.shape[1]
    rows = min(256, keep_ref.shape[0])
    for block in range(keep_ref.shape[0] // rows):
        at = slice(block * rows, (block + 1) * rows)
        outcome = jnp.dot(keep_ref[at, :], weight_ref[:half, :], preferred_element_type=F32)
        outcome = outcome + jnp.dot(rem_ref[at, :], weight_ref[half:, :], preferred_element_type=F32)
        out_ref[at, :] = (hidden_ref[at, :] + outcome).astype(BF16)


def last_mix(hidden, keep, rem, weight):
    rows, width = hidden.shape
    return pl.pallas_call(
        last_kernel,
        out_shape=jax.ShapeDtypeStruct((rows, width), BF16),
        compiler_params=pltpu.CompilerParams(vmem_limit_bytes=VMEM_LIMIT),
        cost_estimate=pl.CostEstimate(flops=2 * rows * 768 * 768, bytes_accessed=rows * 768 * 8, transcendentals=0),
        name="last_mix",
    )(hidden, keep, rem, weight)


def prepare_weights(mix_in, w_up, w_down, mix_out, side):
    blocks, inner = mix_in.shape[0], mix_in.shape[1]
    piece = inner // NB
    half = inner // 2
    eye = jnp.eye(blocks, dtype=mix_in.dtype)
    other = 1 - side

    grid = mix_in.reshape(blocks, inner, 2, 2, piece)
    grid = lax.dynamic_slice_in_dim(jnp.concatenate([grid, grid[:, :, :1]], axis=2), side, 2, axis=2)
    weight_in = jnp.einsum("bisce,bx->biscxe", grid, eye).reshape(blocks * inner, 2 * inner)

    grid = mix_out.reshape(blocks, 2, 2, piece, inner)
    grid = lax.dynamic_slice_in_dim(jnp.concatenate([grid, grid[:, :1]], axis=1), side, 2, axis=1)
    weight_out = jnp.einsum("bscej,bx->scbexj", grid, eye).reshape(2 * inner, blocks * inner)

    def rows(which):
        part = lax.dynamic_slice_in_dim(w_up, which * half, half, axis=1)
        first = jnp.pad(part[0], ((0, 256 - half), (0, 0)))
        second = jnp.pad(part[1], ((256 - half, 0), (0, 0)))
        return jnp.stack([first, second])

    def columns(which):
        part = lax.dynamic_slice_in_dim(w_down, which * half, half, axis=2)
        first = jnp.pad(part[0], ((0, 0), (0, 256 - half)))
        second = jnp.pad(part[1], ((0, 0), (256 - half, 0)))
        return jnp.stack([first, second])

    return weight_in, weight_out, rows(side), rows(other), columns(side), columns(other)


def make_per_device(chunks):
    def per_device(tokens, spectrum, skip, gain, mix_in, w_up, w_down, mix_out):
        groups = lax.axis_size("seq")
        side = lax.axis_index("ch")
        swap = [(0, 1), (1, 0)]
        weight_in, weight_out, up_own, up_rem, down_own, down_send = prepare_weights(
            mix_in, w_up, w_down, mix_out, side
        )
        gain = gain[None, :]
        skip = skip[None, :]
        packed = pack(tokens, spectrum)
        data = lax.all_to_all(packed, "seq", split_axis=0, concat_axis=0, tiled=True)
        convs = convolve(data, make_tables(groups), chunks)
        outs = []
        for q in range(chunks):
            conv = lax.all_to_all(convs[q], "seq", split_axis=0, concat_axis=0, tiled=True)
            hidden, mine = make_hidden(conv, tokens, skip, q, chunks)
            other = lax.ppermute(mine, "ch", swap)
            own, send = first_mix(hidden, mine, other, gain, weight_in)
            rem = lax.ppermute(send, "ch", swap)
            keep, send = mlp(own, rem, up_own, up_rem, down_own, down_send)
            rem = lax.ppermute(send, "ch", swap)
            outs.append(last_mix(hidden, keep, rem, weight_out))
        return outs[0] if chunks == 1 else jnp.concatenate(outs, axis=0)

    return per_device


def solution(mesh):
    return jax.shard_map(
        make_per_device(1),
        mesh=mesh,
        in_specs=(
            P("seq", "ch"),
            P(None, "seq", None, "ch"),
            P("ch"),
            P("ch"),
            P("ch", None, None),
            P("ch", None, None),
            P("ch", None, None),
            P("ch", None, None),
        ),
        out_specs=P("seq", "ch"),
        check_vma=False,
    )
```

```python
import functools
import math

import jax
import jax.numpy as jnp
import ml_dtypes
import numpy as np
from jax import lax
from jax.experimental import pallas as pl
from jax.experimental.pallas import tpu as pltpu
from jax.sharding import PartitionSpec as P

D = 1536
NB = 4
PBLK = 256
QBLK = 512
LANES = 128
F32 = jnp.float32
BF16 = jnp.bfloat16
VMEM_LIMIT = 56 * 1024 * 1024
SMALL_LIMIT = 32 * 1024 * 1024


def dft_numpy(length):
    index = np.arange(length, dtype=np.int64)
    angle = (index[:, None] * index[None, :] % length).astype(np.float32)
    angle = angle * np.float32(2.0 * math.pi / length)
    return (
        np.cos(angle).astype(ml_dtypes.bfloat16).astype(np.float32),
        np.sin(angle).astype(ml_dtypes.bfloat16).astype(np.float32),
    )


def make_tables(groups):
    low = QBLK // groups
    order = (np.arange(groups)[None, :] * low + np.arange(low)[:, None]).reshape(-1)
    cos_long, sin_long = dft_numpy(QBLK)
    cos_long, sin_long = cos_long[order][:, order], sin_long[order][:, order]
    cos_short, sin_short = dft_numpy(PBLK)
    forward = np.concatenate([cos_long, -sin_long], axis=0)
    backward = np.concatenate([cos_long, -sin_long], axis=1) * np.float32(1.0 / (PBLK * QBLK))
    second = np.block([[cos_short, -sin_short], [sin_short, cos_short]])
    third = np.block([[cos_short, sin_short], [-sin_short, cos_short]])
    seq_len = PBLK * QBLK
    angle = (order[:, None].astype(np.int64) * np.arange(PBLK)[None, :] % seq_len).astype(np.float32)
    angle = angle * np.float32(2.0 * math.pi / seq_len)
    half = [t.astype(ml_dtypes.bfloat16) for t in (forward, second, third, backward)]
    return half + [np.cos(angle).astype(np.float32), np.sin(angle).astype(np.float32)]


def pair_split():
    table = np.zeros((2 * LANES, 2 * LANES), np.float32)
    for e in range(2):
        for d in range(LANES):
            table[e * LANES + d, 2 * d + e] = 1.0
    return table.astype(ml_dtypes.bfloat16)


def nt_dot(left, right):
    return lax.dot_general(left, right, (((1,), (1,)), ((), ())), preferred_element_type=F32)


def pack_kernel(tokens_ref, spectrum_ref, split_ref, out_ref, wide):
    split = split_ref[...]
    for block in range(8):
        low, half = block // 2, block % 2
        turned = nt_dot(split, tokens_ref[block * LANES : (block + 1) * LANES, :])
        for e in range(2):
            row = e * 8 + half * 4 + low
            wide[pl.ds(row, LANES, stride=32), :] = turned[e * LANES : (e + 1) * LANES]
    lane = lax.broadcasted_iota(jnp.int32, (LANES, LANES), 0)
    eye = (lane == lax.broadcasted_iota(jnp.int32, (LANES, LANES), 1)).astype(F32).astype(BF16)
    for part in range(2):
        for low in range(4):
            turned = nt_dot(eye, spectrum_ref[part, low])
            for half in range(2):
                row = 16 + part * 8 + half * 4 + low
                wide[pl.ds(row, LANES, stride=32), :] = turned[:, half * LANES : (half + 1) * LANES]
    out_ref[...] = wide[...].reshape(LANES, 32, LANES).astype(BF16)


def pack(tokens, spectrum):
    return pl.pallas_call(
        pack_kernel,
        grid=(3,),
        in_specs=[
            pl.BlockSpec((1024, 256), lambda i: (0, i)),
            pl.BlockSpec((2, 4, 256, LANES), lambda i: (0, 0, 0, i)),
            pl.BlockSpec((256, 256), lambda i: (0, 0)),
        ],
        out_specs=pl.BlockSpec((LANES, 32, LANES), lambda i: (0, i, 0)),
        out_shape=jax.ShapeDtypeStruct((LANES, 96, LANES), BF16),
        scratch_shapes=[pltpu.VMEM((LANES * 32, LANES), F32)],
        compiler_params=pltpu.CompilerParams(vmem_limit_bytes=VMEM_LIMIT),
        cost_estimate=pl.CostEstimate(flops=2 * 10**9, bytes_accessed=6 * 2**20, transcendentals=0),
        name="pack",
    )(tokens, spectrum, pair_split())


def conv_kernel(data_ref, forward_ref, second_ref, third_ref, backward_ref, cos_ref, sin_ref, out_ref, wide, back, outs):
    slot = pl.program_id(0)
    wide[...] = data_ref[...].reshape(LANES * 32, LANES).astype(F32)

    def piece(row):
        return wide[pl.ds(row, LANES, stride=32), :]

    def filters(part):
        return jnp.concatenate(
            [
                jnp.concatenate([piece(16 + part * 8 + half * 4 + low) for half in range(2)], axis=1)
                for low in range(4)
            ],
            axis=0,
        )

    filter_real, filter_imag = filters(0), filters(1)
    for e in range(2):
        block = jnp.concatenate(
            [
                jnp.concatenate([piece(e * 8 + half * 4 + low) for half in range(2)], axis=1).astype(BF16)
                for low in range(4)
            ],
            axis=0,
        )
        first = jnp.dot(forward_ref[...], block, preferred_element_type=F32)
        first_real, first_imag = first[:QBLK], first[QBLK:]
        turn_cos, turn_sin = cos_ref[...], sin_ref[...]
        turned = jnp.concatenate(
            [
                (first_real * turn_cos + first_imag * turn_sin).astype(BF16),
                (first_imag * turn_cos - first_real * turn_sin).astype(BF16),
            ],
            axis=1,
        )
        spectral = jnp.dot(turned, second_ref[...], preferred_element_type=F32)
        spectral_real, spectral_imag = spectral[:, :PBLK], spectral[:, PBLK:]
        filtered = jnp.concatenate(
            [
                (spectral_real * filter_real - spectral_imag * filter_imag).astype(BF16),
                (spectral_real * filter_imag + spectral_imag * filter_real).astype(BF16),
            ],
            axis=1,
        )
        third = jnp.dot(filtered, third_ref[...], preferred_element_type=F32)
        back_real, back_imag = third[:, :PBLK], third[:, PBLK:]
        back[:QBLK, :] = (back_real * turn_cos - back_imag * turn_sin).astype(BF16)
        back[QBLK:, :] = (back_real * turn_sin + back_imag * turn_cos).astype(BF16)
        conv = jnp.dot(backward_ref[...], back[...], preferred_element_type=F32)
        for low in range(4):
            for half in range(2):
                row = (low // 2) * 24 + ((slot * 2 + e) * 2 + half) * 2 + low % 2
                outs[pl.ds(row, LANES, stride=48), :] = conv[
                    low * LANES : (low + 1) * LANES, half * LANES : (half + 1) * LANES
                ]

    @pl.when(slot == 2)
    def _():
        out_ref[...] = outs[...].astype(BF16)


def convolve(data, tables):
    rows = LANES * 48
    whole = lambda shape: pl.BlockSpec(shape, lambda i: (0,) * len(shape))
    return pl.pallas_call(
        conv_kernel,
        grid=(3,),
        in_specs=[pl.BlockSpec((LANES, 32, LANES), lambda i: (0, i, 0))] + [whole(t.shape) for t in tables],
        out_specs=whole((rows, LANES)),
        out_shape=jax.ShapeDtypeStruct((rows, LANES), BF16),
        scratch_shapes=[
            pltpu.VMEM((LANES * 32, LANES), F32),
            pltpu.VMEM((2 * QBLK, PBLK), BF16),
            pltpu.VMEM((rows, LANES), F32),
        ],
        compiler_params=pltpu.CompilerParams(vmem_limit_bytes=VMEM_LIMIT),
        cost_estimate=pl.CostEstimate(flops=64 * 10**8, bytes_accessed=8 * 2**20, transcendentals=0),
        name="convolve",
    )(data, *tables)


def hidden_kernel(
    side_ref, scales_ref, split_ref, conv_hbm, mine_hbm, theirs_hbm, mix_mine, mix_theirs,
    hidden_ref, shuffled_ref, conv_ref, tokens_ref, mix_ref, wide, normed, sems,
):
    side = side_ref[0]
    width = hidden_ref.shape[2]
    count = hidden_ref.shape[1]
    start = pl.multiple_of(side * count, count)
    copies = [
        pltpu.make_async_copy(conv_hbm, conv_ref, sems.at[0]),
        pltpu.make_async_copy(mine_hbm.at[pl.ds(start, count)], tokens_ref.at[0], sems.at[1]),
        pltpu.make_async_copy(theirs_hbm, tokens_ref.at[1], sems.at[2]),
        pltpu.make_async_copy(mix_mine, mix_ref.at[0], sems.at[3]),
        pltpu.make_async_copy(mix_theirs, mix_ref.at[1], sems.at[4]),
    ]
    for copy in copies:
        copy.start()
    split = split_ref[...]
    copies[0].wait()
    wide[...] = conv_ref[...].astype(F32)
    copies[1].wait()
    copies[2].wait()
    for block in range(count // LANES):
        low, half = block // 2, block % 2
        rows = slice(block * LANES, (block + 1) * LANES)
        total = 0.0
        for s in range(2):
            home = side if s == 0 else 1 - side
            pieces = []
            for slot in range(3):
                turned = jnp.concatenate(
                    [
                        wide[pl.ds(home * 24 + ((slot * 2 + e) * 2 + half) * 2 + low, LANES, stride=48), :].T
                        for e in range(2)
                    ],
                    axis=1,
                ).astype(BF16)
                conv = jnp.dot(turned, split, preferred_element_type=F32)
                cols = slice(slot * 256, (slot + 1) * 256)
                values = tokens_ref[s, rows, cols].astype(F32)
                mixed = conv + scales_ref[s, 0:1, cols] * values
                hidden = values + mixed * jax.nn.sigmoid(values)
                hidden_ref[s, rows, cols] = hidden
                pieces.append(jnp.sum(hidden, axis=1, keepdims=True))
            total = total + (pieces[0] + pieces[1] + pieces[2])
        mean = total / (2 * width)
        first = hidden_ref[0, rows, :] - mean
        second = hidden_ref[1, rows, :] - mean
        square = jnp.sum(first * first, axis=1, keepdims=True) + jnp.sum(second * second, axis=1, keepdims=True)
        scale = lax.rsqrt(square / (2 * width) + 1e-05)
        normed[0, rows, :] = (first * scale * scales_ref[0, 1:2, :]).astype(BF16)
        normed[1, rows, :] = (second * scale * scales_ref[1, 1:2, :]).astype(BF16)
    for s in range(2):
        copies[3 + s].wait()
        shuffled_ref[s] = jnp.dot(normed[s], mix_ref[s], preferred_element_type=F32).astype(BF16)


def make_hidden(side, conv, mine, theirs, scales, mix):
    rows = theirs.shape[0]
    return pl.pallas_call(
        hidden_kernel,
        in_specs=[pl.BlockSpec(memory_space=pltpu.SMEM)]
        + [pl.BlockSpec(memory_space=pltpu.VMEM)] * 2
        + [pl.BlockSpec(memory_space=pltpu.HBM)] * 5,
        out_shape=[
            jax.ShapeDtypeStruct((2, rows, 768), F32),
            jax.ShapeDtypeStruct((2, rows, 1024), BF16),
        ],
        scratch_shapes=[
            pltpu.VMEM(conv.shape, BF16),
            pltpu.VMEM((2, rows, 768), BF16),
            pltpu.VMEM((2, 768, 1024), BF16),
            pltpu.VMEM(conv.shape, F32),
            pltpu.VMEM((2, rows, 768), BF16),
            pltpu.SemaphoreType.DMA((5,)),
        ],
        compiler_params=pltpu.CompilerParams(vmem_limit_bytes=SMALL_LIMIT),
        cost_estimate=pl.CostEstimate(flops=3 * 10**9, bytes_accessed=12 * 2**20, transcendentals=10**6),
        name="hidden",
    )(side, scales, pair_split(), conv, mine, theirs, *mix)


def mlp_kernel(
    side_ref, hidden_ref, shuffled_ref, up_mine, up_theirs, down_mine, down_theirs, mix_mine, mix_theirs,
    keep_ref, send_ref, down_buf, gathered,
):
    side = side_ref[0]
    for group, (up_ref, down_ref) in enumerate(((up_mine, down_mine), (up_theirs, down_theirs))):
        home = side if group == 0 else 1 - side
        for c in range(2):
            lanes = pl.multiple_of((2 * home + c) * 256, 256)
            total = 0.0
            for s in range(2):
                start = pl.multiple_of((side if s == 0 else 1 - side) * 192, 192)
                mixed = shuffled_ref[s, :, pl.ds(lanes, 256)][:, :192]
                total = total + jnp.dot(mixed, up_ref[c, pl.ds(start, 192), :], preferred_element_type=F32)
            active = jax.nn.gelu(total, approximate=True).astype(BF16)
            down_buf[...] = jnp.dot(active, down_ref[c], preferred_element_type=F32).astype(BF16)
            for s in range(2):
                start = pl.multiple_of((side if s == 0 else 1 - side) * LANES, LANES)
                gathered[s, :, pl.ds(lanes, 256)] = down_buf[:, pl.ds(start, 256)]
    for s, (ref, mix_ref) in enumerate(((keep_ref, mix_mine), (send_ref, mix_theirs))):
        outcome = jnp.dot(gathered[s], mix_ref[...], preferred_element_type=F32)
        ref[...] = (hidden_ref[s] + outcome).astype(BF16)


def mlp(side, hidden, shuffled, ups, downs, mix, chunk, chunks):
    rows = hidden.shape[1] // chunks
    whole = lambda shape: pl.BlockSpec(shape, lambda i: (0,) * len(shape), pipeline_mode=pl.Buffered(1))
    return pl.pallas_call(
        mlp_kernel,
        grid=(1,),
        in_specs=[
            pl.BlockSpec(memory_space=pltpu.SMEM),
            pl.BlockSpec((2, rows, 768), lambda i: (0, chunk, 0), pipeline_mode=pl.Buffered(1)),
            pl.BlockSpec((2, rows, 1024), lambda i: (0, chunk, 0), pipeline_mode=pl.Buffered(1)),
        ]
        + [whole(w.shape) for w in (*ups, *downs, *mix)],
        out_specs=[whole((rows, 768))] * 2,
        out_shape=[jax.ShapeDtypeStruct((rows, 768), BF16)] * 2,
        scratch_shapes=[pltpu.VMEM((rows, 384), BF16), pltpu.VMEM((2, rows, 1024), BF16)],
        compiler_params=pltpu.CompilerParams(vmem_limit_bytes=SMALL_LIMIT),
        cost_estimate=pl.CostEstimate(
            flops=rows * 14 * 10**6, bytes_accessed=14 * 2**20, transcendentals=rows * 6144
        ),
        name="mlp",
    )(side, hidden, shuffled, *ups, *downs, *mix)


def prepare_kernel(place_ref, in_got, in_passed, out_got, out_passed, first_ref, last_ref):
    home, core = place_ref[0], place_ref[1]
    blocks, inner = in_got.shape[0], in_got.shape[1]
    piece = inner // NB
    spare = 256 - blocks * piece

    def places(shape, axis, offset):
        row = lax.broadcasted_iota(jnp.int32, shape, axis)
        group = sum((row >= c * piece).astype(jnp.int32) for c in range(1, NB))
        target = lax.broadcasted_iota(jnp.int32, shape, 1 - axis)
        return (target == row + group * (256 - piece) + offset).astype(F32).astype(BF16)

    for b in range(blocks):
        weight = jnp.where(core == 0, in_got[b], in_passed[b])
        picked = jnp.dot(weight, places((inner, NB * 256), 0, b * piece), preferred_element_type=F32)
        first_ref[b * inner : (b + 1) * inner, :] = picked.astype(BF16)
        weight = jnp.where(core == 1, out_got[b], out_passed[b])
        offset = b * piece + jnp.where(home == 0, 0, spare)
        picked = jnp.dot(places((NB * 256, inner), 1, offset), weight, preferred_element_type=F32)
        last_ref[:, b * inner : (b + 1) * inner] = picked.astype(BF16)


def prepare(place, in_got, in_passed, out_got, out_passed):
    blocks, inner = in_got.shape[0], in_got.shape[1]
    return pl.pallas_call(
        prepare_kernel,
        in_specs=[pl.BlockSpec(memory_space=pltpu.SMEM)] + [pl.BlockSpec(memory_space=pltpu.VMEM)] * 4,
        out_shape=[
            jax.ShapeDtypeStruct((blocks * inner, NB * 256), BF16),
            jax.ShapeDtypeStruct((NB * 256, blocks * inner), BF16),
        ],
        compiler_params=pltpu.CompilerParams(vmem_limit_bytes=VMEM_LIMIT),
        cost_estimate=pl.CostEstimate(flops=2 * 10**9, bytes_accessed=6 * 2**20, transcendentals=0),
        name="prepare",
    )(place, in_got, in_passed, out_got, out_passed)


def make_per_device(chunks):
    def per_device(tokens, spectrum, skip, gain, mix_in, w_up, w_down, mix_out):
        groups = lax.axis_size("seq")
        both = ("seq", "ch")
        side = lax.axis_index("ch")
        core = lax.axis_index("seq") % 2
        swap = [(0, 1), (1, 0)]
        step = groups // 2

        def near(which):
            return [
                (s * 2 + h, (s ^ step) * 2 + 1 - h) for h in range(2) for s in range(groups) if s % 2 == which
            ]

        def across(which):
            return [(s, s ^ 1) for s in range(groups) if s % 2 == which]

        count = tokens.shape[0] // 2
        place = jnp.stack([side, core]).astype(jnp.int32)
        other_place = jnp.stack([1 - side, core]).astype(jnp.int32)
        packed = pack(tokens, spectrum)
        data = lax.all_to_all(packed, "seq", split_axis=0, concat_axis=0, tiled=True)

        weights, cores = (w_up, w_down, mix_in, mix_out), (0, 1, 0, 1)
        got = [lax.ppermute(w, both, near(which)) for w, which in zip(weights, cores)]
        theirs = lax.ppermute(lax.dynamic_slice_in_dim(tokens, (1 - side) * count, count, axis=0), "ch", swap)
        scales_mine = jnp.stack([skip, gain])
        scales = jnp.stack([scales_mine, lax.ppermute(scales_mine, "ch", swap)])
        first_mine, last_mine = prepare(place, mix_in, mix_in, mix_out, mix_out)
        data, first_mine, last_mine, theirs, scales = lax.optimization_barrier(
            (data, first_mine, last_mine, theirs, scales)
        )
        conv = convolve(data, make_tables(groups))

        conv, *got = lax.optimization_barrier((conv, *got))
        conv = lax.all_to_all(conv, both, split_axis=0, concat_axis=0, tiled=True)
        passed = [lax.ppermute(g, "seq", across(which)) for g, which in zip(got, cores)]
        up_theirs, down_theirs = (jnp.where(core == cores[i], got[i], passed[i]) for i in range(2))
        first_theirs, last_theirs = prepare(other_place, got[2], passed[2], got[3], passed[3])
        mix_first = (first_mine, first_theirs)
        mix_last = (last_mine, last_theirs)
        hidden, shuffled = make_hidden(place, conv, tokens, theirs, scales, mix_first)
        out = jnp.zeros(tokens.shape, tokens.dtype)
        rows = count // chunks
        for q in range(chunks):
            keep, send = mlp(place, hidden, shuffled, (w_up, up_theirs), (w_down, down_theirs), mix_last, q, chunks)
            sent = lax.ppermute(send, "ch", swap)
            out = lax.dynamic_update_slice_in_dim(out, keep, side * count + q * rows, axis=0)
            out = lax.dynamic_update_slice_in_dim(out, sent, (1 - side) * count + q * rows, axis=0)
        return out

    return per_device


def solution(mesh):
    return jax.shard_map(
        make_per_device(2),
        mesh=mesh,
        in_specs=(
            P("seq", "ch"),
            P(None, "seq", None, "ch"),
            P("ch"),
            P("ch"),
            P("ch", None, None),
            P("ch", None, None),
            P("ch", None, None),
            P("ch", None, None),
        ),
        out_specs=P("seq", "ch"),
        check_vma=False,
    )
```

```python
import functools
import math

import jax
import jax.numpy as jnp
import ml_dtypes
import numpy as np
from jax import lax
from jax.experimental import pallas as pl
from jax.experimental.pallas import tpu as pltpu
from jax.sharding import PartitionSpec as P

D = 1536
NB = 4
PBLK = 256
QBLK = 512
LANES = 128
F32 = jnp.float32
BF16 = jnp.bfloat16
VMEM_LIMIT = 56 * 1024 * 1024
SMALL_LIMIT = 32 * 1024 * 1024
CONV_LIMIT = 40 * 1024 * 1024


def dft_numpy(length):
    index = np.arange(length, dtype=np.int64)
    angle = (index[:, None] * index[None, :] % length).astype(np.float32)
    angle = angle * np.float32(2.0 * math.pi / length)
    return (
        np.cos(angle).astype(ml_dtypes.bfloat16).astype(np.float32),
        np.sin(angle).astype(ml_dtypes.bfloat16).astype(np.float32),
    )


def make_tables(groups):
    low = QBLK // groups
    order = (np.arange(groups)[None, :] * low + np.arange(low)[:, None]).reshape(-1)
    cos_long, sin_long = dft_numpy(QBLK)
    cos_long, sin_long = cos_long[order][:, order], sin_long[order][:, order]
    cos_short, sin_short = dft_numpy(PBLK)
    second = np.block([[cos_short, -sin_short], [sin_short, cos_short]])
    third = np.block([[cos_short, sin_short], [-sin_short, cos_short]])
    seq_len = PBLK * QBLK
    angle = (order[:, None].astype(np.int64) * np.arange(PBLK)[None, :] % seq_len).astype(np.float32)
    angle = angle * np.float32(2.0 * math.pi / seq_len)
    half = [t.astype(ml_dtypes.bfloat16) for t in (cos_long, -sin_long, second, third)]
    return half + [np.cos(angle).astype(np.float32), np.sin(angle).astype(np.float32)]


def pair_split(pairs):
    table = np.zeros((2 * pairs, 2 * pairs), np.float32)
    for e in range(2):
        for d in range(pairs):
            table[e * pairs + d, 2 * d + e] = 1.0
    return table.astype(ml_dtypes.bfloat16)


def nt_dot(left, right):
    return lax.dot_general(left, right, (((1,), (1,)), ((), ())), preferred_element_type=F32)


def pack_kernel(tokens_ref, spectrum_ref, split_ref, out_ref, wide):
    split = split_ref[...]
    count = split.shape[0] // 2
    for low in range(4):
        turned = nt_dot(split, tokens_ref[low * 256 : (low + 1) * 256, :])
        for e in range(2):
            for half in range(2):
                wide[e * 8 + half * 4 + low] = turned[
                    e * count : (e + 1) * count, half * LANES : (half + 1) * LANES
                ]
    row = lax.broadcasted_iota(jnp.int32, (count, LANES), 0)
    pick = (row == lax.broadcasted_iota(jnp.int32, (count, LANES), 1)).astype(F32).astype(BF16)
    for part in range(2):
        for low in range(4):
            turned = nt_dot(pick, spectrum_ref[part, low])
            for half in range(2):
                wide[16 + part * 8 + half * 4 + low] = turned[:, half * LANES : (half + 1) * LANES]
    out_ref[...] = jnp.swapaxes(wide[...], 0, 1).astype(BF16)


def pack(tokens, spectrum):
    count = LANES
    return pl.pallas_call(
        pack_kernel,
        grid=(3,),
        in_specs=[
            pl.BlockSpec((1024, 2 * LANES), lambda i: (0, i)),
            pl.BlockSpec((2, 4, 256, LANES), lambda i: (0, 0, 0, i)),
            pl.BlockSpec((2 * LANES, 2 * LANES), lambda i: (0, 0)),
        ],
        out_specs=pl.BlockSpec((count, 32, LANES), lambda i: (0, i, 0)),
        out_shape=jax.ShapeDtypeStruct((LANES, 96, LANES), BF16),
        scratch_shapes=[pltpu.VMEM((32, count, LANES), F32)],
        compiler_params=pltpu.CompilerParams(vmem_limit_bytes=VMEM_LIMIT),
        cost_estimate=pl.CostEstimate(flops=2 * 10**9, bytes_accessed=6 * 2**20, transcendentals=0),
        name="pack",
    )(tokens, spectrum, pair_split(count))


def conv_kernel(data_hbm, *rest):
    sources, (out_hbm, data, wide, back, outs, sems, table_sems, out_sems), tables = rest[:6], rest[6:14], rest[14:]
    cos_long_ref, sin_long_ref, second_ref, third_ref, cos_ref, sin_ref, staged = tables

    def fetch(slot):
        rows = pl.ds(pl.multiple_of(slot * 32, 32), 32)
        return pltpu.make_async_copy(data_hbm.at[:, rows, :], data.at[slot], sems.at[slot])

    loads = [pltpu.make_async_copy(sources[i], tables[i], table_sems.at[i]) for i in range(6)]
    fetch(0).start()
    for i in (0, 1, 4, 5, 2, 3):
        loads[i].start()
    fetch(1).start()
    fetch(2).start()

    def filters(part):
        return jnp.concatenate(
            [
                jnp.concatenate([wide[16 + part * 8 + half * 4 + low] for half in range(2)], axis=1)
                for low in range(4)
            ],
            axis=0,
        )

    @pl.loop(0, 3)
    def _(slot):
        fetch(slot).wait()
        for part in range(4):
            at = slice(part * 32, (part + 1) * 32)
            wide[:, at, :] = jnp.swapaxes(data[slot, at].astype(F32), 0, 1)

        @pl.when(slot == 0)
        def _():
            for load in loads:
                load.wait()

        channels = range(2)
        blocks = [
            jnp.concatenate(
                [
                    jnp.concatenate([wide[e * 8 + half * 4 + low] for half in range(2)], axis=1).astype(BF16)
                    for low in range(4)
                ],
                axis=0,
            )
            for e in channels
        ]
        turn_cos, turn_sin = cos_ref[...], sin_ref[...]
        first_real = [jnp.dot(cos_long_ref[...], block, preferred_element_type=F32) for block in blocks]
        first_imag = [jnp.dot(sin_long_ref[...], block, preferred_element_type=F32) for block in blocks]
        turned = [
            jnp.concatenate(
                [
                    (first_real[e] * turn_cos + first_imag[e] * turn_sin).astype(BF16),
                    (first_imag[e] * turn_cos - first_real[e] * turn_sin).astype(BF16),
                ],
                axis=1,
            )
            for e in channels
        ]
        spectral = [jnp.dot(turned[e], second_ref[...], preferred_element_type=F32) for e in channels]
        filter_real, filter_imag = filters(0), filters(1)
        filtered = [
            jnp.concatenate(
                [
                    (spectral[e][:, :PBLK] * filter_real - spectral[e][:, PBLK:] * filter_imag).astype(BF16),
                    (spectral[e][:, :PBLK] * filter_imag + spectral[e][:, PBLK:] * filter_real).astype(BF16),
                ],
                axis=1,
            )
            for e in channels
        ]
        third = [jnp.dot(filtered[e], third_ref[...], preferred_element_type=F32) for e in channels]
        for e in channels:
            back_real, back_imag = third[e][:, :PBLK], third[e][:, PBLK:]
            back[e, 0] = (back_real * turn_cos - back_imag * turn_sin).astype(BF16)
            back[e, 1] = (back_real * turn_sin + back_imag * turn_cos).astype(BF16)
        for e in channels:
            conv = jnp.dot(cos_long_ref[...], back[e, 0], preferred_element_type=F32)
            conv = conv + jnp.dot(sin_long_ref[...], back[e, 1], preferred_element_type=F32)
            conv = conv * (1.0 / (PBLK * QBLK))
            for low in range(4):
                for half in range(2):
                    row = (low // 2) * 24 + ((slot * 2 + e) * 2 + half) * 2 + low % 2
                    outs[row] = conv[low * LANES : (low + 1) * LANES, half * LANES : (half + 1) * LANES]

    stores = []
    for part in range(4):
        at = slice(part * 32, (part + 1) * 32)
        staged[at] = jnp.swapaxes(outs[:, at, :], 0, 1).astype(BF16)
        stores.append(pltpu.make_async_copy(staged.at[at], out_hbm.at[at], out_sems.at[part]))
        stores[-1].start()
    for store in stores:
        store.wait()


def convolve(data, tables):
    in_hbm = lambda x: pltpu.with_memory_space_constraint(x, pltpu.HBM)
    return pl.pallas_call(
        conv_kernel,
        in_specs=[pl.BlockSpec(memory_space=pltpu.HBM)] * (1 + len(tables)),
        out_specs=pl.BlockSpec(memory_space=pltpu.HBM),
        out_shape=pltpu.HBM((LANES, 48, LANES), BF16),
        scratch_shapes=[
            pltpu.VMEM((3, LANES, 32, LANES), BF16),
            pltpu.VMEM((32, LANES, LANES), F32),
            pltpu.VMEM((2, 2, QBLK, PBLK), BF16),
            pltpu.VMEM((48, LANES, LANES), F32),
            pltpu.SemaphoreType.DMA((3,)),
            pltpu.SemaphoreType.DMA((6,)),
            pltpu.SemaphoreType.DMA((4,)),
        ]
        + [pltpu.VMEM(t.shape, t.dtype) for t in tables]
        + [pltpu.VMEM((LANES, 48, LANES), BF16)],
        compiler_params=pltpu.CompilerParams(vmem_limit_bytes=CONV_LIMIT),
        cost_estimate=pl.CostEstimate(flops=64 * 10**8, bytes_accessed=8 * 2**20, transcendentals=0),
        name="convolve",
    )(*(in_hbm(x) for x in (data, *tables))).reshape(LANES * 48, LANES)


def hidden_kernel(
    side_ref, scales_ref, split_ref, mix_mine, mix_theirs, conv_hbm, mine_hbm, theirs_hbm,
    hidden_ref, shuffled_ref, conv_ref, tokens_ref, mix_ref, wide, normed, sems, conv_sems,
):
    side = side_ref[0]
    width = hidden_ref.shape[2]
    count = hidden_ref.shape[1]
    start = pl.multiple_of(side * count, count)
    quarter = conv_hbm.shape[0] // 4
    arrivals = []
    for part in range(4):
        at = slice(part * quarter, (part + 1) * quarter)
        arrivals.append(pltpu.make_async_copy(conv_hbm.at[at], conv_ref.at[at], conv_sems.at[part]))
        arrivals[-1].start()
    copies = [
        pltpu.make_async_copy(mine_hbm.at[pl.ds(start, count)], tokens_ref.at[0], sems.at[0]),
        pltpu.make_async_copy(theirs_hbm, tokens_ref.at[1], sems.at[1]),
        pltpu.make_async_copy(mix_mine, mix_ref.at[0], sems.at[2]),
        pltpu.make_async_copy(mix_theirs, mix_ref.at[1], sems.at[3]),
    ]
    copies[0].start()
    copies[1].start()
    split = split_ref[...]
    for part in range(4):
        at = slice(part * quarter, (part + 1) * quarter)
        arrivals[part].wait()
        wide[:, at, :] = jnp.swapaxes(conv_ref[at].astype(F32), 0, 1)
    copies[2].start()
    copies[3].start()
    copies[0].wait()
    copies[1].wait()
    for block in range(count // LANES):
        low, half = block // 2, block % 2
        rows = slice(block * LANES, (block + 1) * LANES)
        total = 0.0
        for s in range(2):
            home = side if s == 0 else 1 - side
            pieces = []
            for slot in range(3):
                turned = jnp.concatenate(
                    [
                        wide[home * 24 + ((slot * 2 + e) * 2 + half) * 2 + low].T
                        for e in range(2)
                    ],
                    axis=1,
                ).astype(BF16)
                conv = jnp.dot(turned, split, preferred_element_type=F32)
                cols = slice(slot * 256, (slot + 1) * 256)
                values = tokens_ref[s, rows, cols].astype(F32)
                mixed = conv + scales_ref[s, 0:1, cols] * values
                hidden = values + mixed * jax.nn.sigmoid(values)
                hidden_ref[s, rows, cols] = hidden
                pieces.append(jnp.sum(hidden, axis=1, keepdims=True))
            total = total + (pieces[0] + pieces[1] + pieces[2])
        mean = total / (2 * width)
        first = hidden_ref[0, rows, :] - mean
        second = hidden_ref[1, rows, :] - mean
        square = jnp.sum(first * first, axis=1, keepdims=True) + jnp.sum(second * second, axis=1, keepdims=True)
        scale = lax.rsqrt(square / (2 * width) + 1e-05)
        normed[0, rows, :] = (first * scale * scales_ref[0, 1:2, :]).astype(BF16)
        normed[1, rows, :] = (second * scale * scales_ref[1, 1:2, :]).astype(BF16)
    for s in range(2):
        copies[2 + s].wait()
        shuffled_ref[s] = jnp.dot(normed[s], mix_ref[s], preferred_element_type=F32).astype(BF16)


def make_hidden(side, conv, mine, theirs, scales, mix):
    rows = theirs.shape[0]
    conv = conv.reshape(LANES, 48, LANES)
    return pl.pallas_call(
        hidden_kernel,
        in_specs=[pl.BlockSpec(memory_space=pltpu.SMEM)]
        + [pl.BlockSpec(memory_space=pltpu.VMEM)] * 2
        + [pl.BlockSpec(memory_space=pltpu.HBM)] * 5,
        out_shape=[
            jax.ShapeDtypeStruct((2, rows, 768), F32),
            jax.ShapeDtypeStruct((2, rows, 1024), BF16),
        ],
        scratch_shapes=[
            pltpu.VMEM(conv.shape, BF16),
            pltpu.VMEM((2, rows, 768), BF16),
            pltpu.VMEM((2, *mix[0].shape), BF16),
            pltpu.VMEM((48, LANES, LANES), F32),
            pltpu.VMEM((2, rows, 768), BF16),
            pltpu.SemaphoreType.DMA((4,)),
            pltpu.SemaphoreType.DMA((4,)),
        ],
        compiler_params=pltpu.CompilerParams(vmem_limit_bytes=SMALL_LIMIT),
        cost_estimate=pl.CostEstimate(flops=3 * 10**9, bytes_accessed=12 * 2**20, transcendentals=10**6),
        name="hidden",
    )(
        side,
        scales,
        pair_split(LANES),
        *(pltpu.with_memory_space_constraint(x, pltpu.HBM) for x in (*mix, conv, mine, theirs)),
    )


def mlp_kernel(
    first_row, side_ref, hidden_ref, shuffled_ref, up_mine, up_theirs, down_mine, down_theirs, mix_mine, mix_theirs,
    keep_ref, send_ref, down_buf, gathered,
):
    side = side_ref[0]
    rows = slice(first_row, first_row + keep_ref.shape[0])
    for group, (up_ref, down_ref) in enumerate(((up_mine, down_mine), (up_theirs, down_theirs))):
        home = side if group == 0 else 1 - side
        for c in range(2):
            lanes = pl.multiple_of((2 * home + c) * 256, 256)
            total = 0.0
            for s in range(2):
                start = pl.multiple_of((side if s == 0 else 1 - side) * 192, 192)
                mixed = shuffled_ref[s, rows, pl.ds(lanes, 256)][:, :192]
                total = total + jnp.dot(mixed, up_ref[c, pl.ds(start, 192), :], preferred_element_type=F32)
            active = jax.nn.gelu(total, approximate=True).astype(BF16)
            down_buf[...] = jnp.dot(active, down_ref[c], preferred_element_type=F32).astype(BF16)
            for s in range(2):
                start = pl.multiple_of((side if s == 0 else 1 - side) * LANES, LANES)
                gathered[s, :, pl.ds(lanes, 256)] = down_buf[:, pl.ds(start, 256)]
    for s, (ref, mix_ref) in enumerate(((keep_ref, mix_mine), (send_ref, mix_theirs))):
        outcome = jnp.dot(gathered[s], mix_ref[...], preferred_element_type=F32)
        ref[...] = (hidden_ref[s, rows, :] + outcome).astype(BF16)


def mlp(side, hidden, shuffled, ups, downs, mix, first_row, rows):
    return pl.pallas_call(
        functools.partial(mlp_kernel, first_row),
        in_specs=[pl.BlockSpec(memory_space=pltpu.SMEM)] + [pl.BlockSpec(memory_space=pltpu.VMEM)] * 8,
        out_shape=[jax.ShapeDtypeStruct((rows, 768), BF16)] * 2,
        scratch_shapes=[pltpu.VMEM((rows, 384), BF16), pltpu.VMEM((2, rows, 1024), BF16)],
        compiler_params=pltpu.CompilerParams(vmem_limit_bytes=SMALL_LIMIT),
        cost_estimate=pl.CostEstimate(
            flops=rows * 14 * 10**6, bytes_accessed=14 * 2**20, transcendentals=rows * 6144
        ),
        name="mlp",
    )(side, hidden, shuffled, *ups, *downs, *mix)


def choose(place_ref, want, got, passed, target, sem, begin):
    for core, source in ((want, got), (1 - want, passed)):
        @pl.when(place_ref[1] == core)
        def _():
            copy = pltpu.make_async_copy(source, target, sem)
            copy.start() if begin else copy.wait()


def places(shape, axis, offset, piece):
    row = lax.broadcasted_iota(jnp.int32, shape, axis)
    group = sum((row >= c * piece).astype(jnp.int32) for c in range(1, NB))
    target = lax.broadcasted_iota(jnp.int32, shape, 1 - axis)
    return (target == row + group * (256 - piece) + offset).astype(F32).astype(BF16)


def rearrange(home, b, weight_in, weight_out, first_ref, last_ref):
    inner = weight_in.shape[0]
    piece = inner // NB
    picked = jnp.dot(weight_in, places((inner, NB * 256), 0, b * piece, piece), preferred_element_type=F32)
    first_ref[b * inner : (b + 1) * inner, :] = picked.astype(BF16)
    offset = b * piece + jnp.where(home == 0, 0, 256 - 2 * piece)
    picked = jnp.dot(places((NB * 256, inner), 1, offset, piece), weight_out, preferred_element_type=F32)
    last_ref[:, b * inner : (b + 1) * inner] = picked.astype(BF16)


def prepare_mine_kernel(place_ref, in_ref, out_ref, first_ref, last_ref):
    for b in range(in_ref.shape[0]):
        rearrange(place_ref[0], b, in_ref[b], out_ref[b], first_ref, last_ref)


def prepare_theirs_kernel(
    place_ref, in_got, in_passed, out_got, out_passed, up_got, up_passed, down_got, down_passed,
    first_ref, last_ref, up_theirs, down_theirs, in_ref, out_ref, up_ref, down_ref, sems,
):
    picks = [
        (0, in_got, in_passed, in_ref, sems.at[0]),
        (1, out_got, out_passed, out_ref, sems.at[1]),
        (0, up_got, up_passed, up_ref, sems.at[2]),
        (1, down_got, down_passed, down_ref, sems.at[3]),
    ]
    for pick in picks:
        choose(place_ref, *pick, True)
    choose(place_ref, *picks[0], False)
    choose(place_ref, *picks[1], False)
    for b in range(in_ref.shape[0]):
        rearrange(1 - place_ref[0], b, in_ref[b], out_ref[b], first_ref, last_ref)
    choose(place_ref, *picks[2], False)
    choose(place_ref, *picks[3], False)
    stores = [
        pltpu.make_async_copy(up_ref, up_theirs, sems.at[4]),
        pltpu.make_async_copy(down_ref, down_theirs, sems.at[5]),
    ]
    for store in stores:
        store.start()
    for store in stores:
        store.wait()


def prepare_shapes(blocks, inner):
    return [
        jax.ShapeDtypeStruct((blocks * inner, NB * 256), BF16),
        jax.ShapeDtypeStruct((NB * 256, blocks * inner), BF16),
    ]


def prepare_mine(place, mix_in, mix_out):
    return pl.pallas_call(
        prepare_mine_kernel,
        in_specs=[pl.BlockSpec(memory_space=pltpu.SMEM)] + [pl.BlockSpec(memory_space=pltpu.VMEM)] * 2,
        out_specs=[pl.BlockSpec(memory_space=pltpu.VMEM)] * 2,
        out_shape=prepare_shapes(mix_in.shape[0], mix_in.shape[1]),
        compiler_params=pltpu.CompilerParams(vmem_limit_bytes=SMALL_LIMIT),
        cost_estimate=pl.CostEstimate(flops=10**9, bytes_accessed=2**20, transcendentals=0),
        name="prepare_mine",
    )(place, mix_in, mix_out)


def prepare_theirs(place, pairs):
    mix_in, mix_out = pairs[0][0], pairs[1][0]
    arrays = [x for pair in pairs for x in pair]
    return pl.pallas_call(
        prepare_theirs_kernel,
        in_specs=[pl.BlockSpec(memory_space=pltpu.SMEM)] + [pl.BlockSpec(memory_space=pltpu.HBM)] * len(arrays),
        out_specs=[pl.BlockSpec(memory_space=pltpu.VMEM)] * 2 + [pl.BlockSpec(memory_space=pltpu.HBM)] * 2,
        out_shape=prepare_shapes(mix_in.shape[0], mix_in.shape[1])
        + [pltpu.HBM(pair[0].shape, BF16) for pair in pairs[2:]],
        scratch_shapes=[
            pltpu.VMEM(mix_in.shape, BF16),
            pltpu.VMEM(mix_out.shape, BF16),
            pltpu.VMEM(pairs[2][0].shape, BF16),
            pltpu.VMEM(pairs[3][0].shape, BF16),
            pltpu.SemaphoreType.DMA((6,)),
        ],
        compiler_params=pltpu.CompilerParams(vmem_limit_bytes=VMEM_LIMIT),
        cost_estimate=pl.CostEstimate(flops=10**6, bytes_accessed=2**16, transcendentals=0),
        name="prepare_theirs",
    )(place, *(pltpu.with_memory_space_constraint(x, pltpu.HBM) for x in arrays))


def make_per_device(chunks):
    def per_device(tokens, spectrum, skip, gain, mix_in, w_up, w_down, mix_out):
        groups = lax.axis_size("seq")
        both = ("seq", "ch")
        side = lax.axis_index("ch")
        core = lax.axis_index("seq") % 2
        swap = [(0, 1), (1, 0)]
        step = groups // 2

        def near(which):
            return [
                (s * 2 + h, (s ^ step) * 2 + 1 - h) for h in range(2) for s in range(groups) if s % 2 == which
            ]

        def across(which):
            return [(s, s ^ 1) for s in range(groups) if s % 2 == which]

        count = tokens.shape[0] // 2
        place = jnp.stack([side, core]).astype(jnp.int32)
        packed = pack(tokens, spectrum)
        data = lax.all_to_all(packed, "seq", split_axis=0, concat_axis=0, tiled=True)

        weights, cores = (w_up, w_down, mix_in, mix_out), (0, 1, 0, 1)
        got = [lax.ppermute(w, both, near(which)) for w, which in zip(weights, cores)]
        theirs = lax.ppermute(lax.dynamic_slice_in_dim(tokens, (1 - side) * count, count, axis=0), "ch", swap)
        scales_mine = jnp.stack([skip, gain])
        scales = jnp.stack([scales_mine, lax.ppermute(scales_mine, "ch", swap)])
        first_mine, last_mine = prepare_mine(place, mix_in, mix_out)
        tables = [jnp.asarray(t) for t in make_tables(groups)]
        data, first_mine, last_mine, theirs, scales, tables = lax.optimization_barrier(
            (data, first_mine, last_mine, theirs, scales, tables)
        )
        conv = convolve(data, tables)

        conv, got = lax.optimization_barrier((conv, got))
        conv = lax.all_to_all(conv, both, split_axis=0, concat_axis=0, tiled=True)
        passed = [lax.ppermute(g, "seq", across(which)) for g, which in zip(got, cores)]
        pairs = [(got[i], passed[i]) for i in (2, 3, 0, 1)]
        first_theirs, last_theirs, up_theirs, down_theirs = prepare_theirs(place, pairs)
        mix_first = (first_mine, first_theirs)
        mix_last = (last_mine, last_theirs)
        hidden, shuffled = make_hidden(place, conv, tokens, theirs, scales, mix_first)
        out = jnp.zeros(tokens.shape, tokens.dtype)
        rows = count // chunks
        for q in range(chunks):
            keep, send = mlp(
                place, hidden, shuffled, (w_up, up_theirs), (w_down, down_theirs), mix_last, q * rows, rows
            )
            sent = lax.ppermute(send, "ch", swap)
            out = lax.dynamic_update_slice_in_dim(out, keep, side * count + q * rows, axis=0)
            out = lax.dynamic_update_slice_in_dim(out, sent, (1 - side) * count + q * rows, axis=0)
        return out

    return per_device


def solution(mesh):
    return jax.shard_map(
        make_per_device(2),
        mesh=mesh,
        in_specs=(
            P("seq", "ch"),
            P(None, "seq", None, "ch"),
            P("ch"),
            P("ch"),
            P("ch", None, None),
            P("ch", None, None),
            P("ch", None, None),
            P("ch", None, None),
        ),
        out_specs=P("seq", "ch"),
        check_vma=False,
    )
```

```python
import functools
import math

import jax
import jax.numpy as jnp
import ml_dtypes
import numpy as np
from jax import lax
from jax.experimental import pallas as pl
from jax.experimental.pallas import tpu as pltpu
from jax.sharding import PartitionSpec as P

D = 1536
NB = 4
PBLK = 256
QBLK = 512
LANES = 128
F32 = jnp.float32
BF16 = jnp.bfloat16
VMEM_LIMIT = 56 * 1024 * 1024
SMALL_LIMIT = 32 * 1024 * 1024
CONV_LIMIT = 40 * 1024 * 1024


def dft_numpy(length):
    index = np.arange(length, dtype=np.int64)
    angle = (index[:, None] * index[None, :] % length).astype(np.float32)
    angle = angle * np.float32(2.0 * math.pi / length)
    return (
        np.cos(angle).astype(ml_dtypes.bfloat16).astype(np.float32),
        np.sin(angle).astype(ml_dtypes.bfloat16).astype(np.float32),
    )


def make_tables(groups):
    low = QBLK // groups
    order = (np.arange(groups)[None, :] * low + np.arange(low)[:, None]).reshape(-1)
    cos_long, sin_long = dft_numpy(QBLK)
    cos_long, sin_long = cos_long[order][:, order], sin_long[order][:, order]
    cos_short, sin_short = dft_numpy(PBLK)
    second = np.block([[cos_short, -sin_short], [sin_short, cos_short]])
    third = np.block([[cos_short, sin_short], [-sin_short, cos_short]])
    seq_len = PBLK * QBLK
    angle = (order[:, None].astype(np.int64) * np.arange(PBLK)[None, :] % seq_len).astype(np.float32)
    angle = angle * np.float32(2.0 * math.pi / seq_len)
    half = [t.astype(ml_dtypes.bfloat16) for t in (cos_long, -sin_long, second, third)]
    return half + [np.cos(angle).astype(np.float32), np.sin(angle).astype(np.float32)]


def pair_split(pairs):
    table = np.zeros((2 * pairs, 2 * pairs), np.float32)
    for e in range(2):
        for d in range(pairs):
            table[e * pairs + d, 2 * d + e] = 1.0
    return table.astype(ml_dtypes.bfloat16)


def nt_dot(left, right):
    return lax.dot_general(left, right, (((1,), (1,)), ((), ())), preferred_element_type=F32)


def pack_kernel(tokens_ref, spectrum_ref, split_ref, out_ref, wide):
    split = split_ref[...]
    count = split.shape[0] // 2
    for low in range(4):
        turned = nt_dot(split, tokens_ref[low * 256 : (low + 1) * 256, :])
        for e in range(2):
            for half in range(2):
                wide[e * 8 + half * 4 + low] = turned[
                    e * count : (e + 1) * count, half * LANES : (half + 1) * LANES
                ]
    row = lax.broadcasted_iota(jnp.int32, (count, LANES), 0)
    pick = (row == lax.broadcasted_iota(jnp.int32, (count, LANES), 1)).astype(F32).astype(BF16)
    for part in range(2):
        for low in range(4):
            turned = nt_dot(pick, spectrum_ref[part, low])
            for half in range(2):
                wide[16 + part * 8 + half * 4 + low] = turned[:, half * LANES : (half + 1) * LANES]
    out_ref[...] = jnp.swapaxes(wide[...], 0, 1).astype(BF16)


def pack(tokens, spectrum):
    count = LANES
    return pl.pallas_call(
        pack_kernel,
        grid=(3,),
        in_specs=[
            pl.BlockSpec((1024, 2 * LANES), lambda i: (0, i)),
            pl.BlockSpec((2, 4, 256, LANES), lambda i: (0, 0, 0, i)),
            pl.BlockSpec((2 * LANES, 2 * LANES), lambda i: (0, 0)),
        ],
        out_specs=pl.BlockSpec((count, 32, LANES), lambda i: (0, i, 0)),
        out_shape=jax.ShapeDtypeStruct((LANES, 96, LANES), BF16),
        scratch_shapes=[pltpu.VMEM((32, count, LANES), F32)],
        compiler_params=pltpu.CompilerParams(vmem_limit_bytes=VMEM_LIMIT),
        cost_estimate=pl.CostEstimate(flops=2 * 10**9, bytes_accessed=6 * 2**20, transcendentals=0),
        name="pack",
    )(tokens, spectrum, pair_split(count))


def conv_kernel(data_hbm, *rest):
    sources, (out_hbm, data, wide, back, outs, sems, table_sems, out_sems), tables = rest[:6], rest[6:14], rest[14:]
    cos_long_ref, sin_long_ref, second_ref, third_ref, cos_ref, sin_ref, staged = tables

    def fetch(slot):
        rows = pl.ds(slot * 32, 32)
        return pltpu.make_async_copy(data_hbm.at[:, rows, :], data.at[slot], sems.at[slot])

    loads = [pltpu.make_async_copy(sources[i], tables[i], table_sems.at[i]) for i in range(6)]
    fetch(0).start()
    for i in (0, 1, 4, 5, 2, 3):
        loads[i].start()
    fetch(1).start()
    fetch(2).start()

    def filters(now, part):
        return jnp.concatenate(
            [
                jnp.concatenate([wide[now, 16 + part * 8 + half * 4 + low] for half in range(2)], axis=1)
                for low in range(4)
            ],
            axis=0,
        )

    for slot in range(3):
        now = slot % 2
        fetch(slot).wait()
        for part in range(4):
            at = slice(part * 32, (part + 1) * 32)
            wide[now, :, at, :] = jnp.swapaxes(data[slot, at].astype(F32), 0, 1)
        if slot == 0:
            for load in loads:
                load.wait()
        channels = range(2)
        blocks = [
            jnp.concatenate(
                [
                    jnp.concatenate([wide[now, e * 8 + half * 4 + low] for half in range(2)], axis=1).astype(BF16)
                    for low in range(4)
                ],
                axis=0,
            )
            for e in channels
        ]
        turn_cos, turn_sin = cos_ref[...], sin_ref[...]
        first_real = [jnp.dot(cos_long_ref[...], block, preferred_element_type=F32) for block in blocks]
        first_imag = [jnp.dot(sin_long_ref[...], block, preferred_element_type=F32) for block in blocks]
        turned = [
            jnp.concatenate(
                [
                    (first_real[e] * turn_cos + first_imag[e] * turn_sin).astype(BF16),
                    (first_imag[e] * turn_cos - first_real[e] * turn_sin).astype(BF16),
                ],
                axis=1,
            )
            for e in channels
        ]
        spectral = [jnp.dot(turned[e], second_ref[...], preferred_element_type=F32) for e in channels]
        filter_real, filter_imag = filters(now, 0), filters(now, 1)
        filtered = [
            jnp.concatenate(
                [
                    (spectral[e][:, :PBLK] * filter_real - spectral[e][:, PBLK:] * filter_imag).astype(BF16),
                    (spectral[e][:, :PBLK] * filter_imag + spectral[e][:, PBLK:] * filter_real).astype(BF16),
                ],
                axis=1,
            )
            for e in channels
        ]
        third = [jnp.dot(filtered[e], third_ref[...], preferred_element_type=F32) for e in channels]
        for e in channels:
            back_real, back_imag = third[e][:, :PBLK], third[e][:, PBLK:]
            back[e, 0] = (back_real * turn_cos - back_imag * turn_sin).astype(BF16)
            back[e, 1] = (back_real * turn_sin + back_imag * turn_cos).astype(BF16)
        for e in channels:
            conv = jnp.dot(cos_long_ref[...], back[e, 0], preferred_element_type=F32)
            conv = conv + jnp.dot(sin_long_ref[...], back[e, 1], preferred_element_type=F32)
            conv = conv * (1.0 / (PBLK * QBLK))
            for low in range(4):
                for half in range(2):
                    row = (low // 2) * 24 + ((slot * 2 + e) * 2 + half) * 2 + low % 2
                    outs[row] = conv[low * LANES : (low + 1) * LANES, half * LANES : (half + 1) * LANES]

    stores = []
    for part in range(4):
        at = slice(part * 32, (part + 1) * 32)
        staged[at] = jnp.swapaxes(outs[:, at, :], 0, 1).astype(BF16)
        stores.append(pltpu.make_async_copy(staged.at[at], out_hbm.at[at], out_sems.at[part]))
        stores[-1].start()
    for store in stores:
        store.wait()


def convolve(data, tables):
    in_hbm = lambda x: pltpu.with_memory_space_constraint(x, pltpu.HBM)
    return pl.pallas_call(
        conv_kernel,
        in_specs=[pl.BlockSpec(memory_space=pltpu.HBM)] * (1 + len(tables)),
        out_specs=pl.BlockSpec(memory_space=pltpu.HBM),
        out_shape=pltpu.HBM((LANES, 48, LANES), BF16),
        scratch_shapes=[
            pltpu.VMEM((3, LANES, 32, LANES), BF16),
            pltpu.VMEM((2, 32, LANES, LANES), F32),
            pltpu.VMEM((2, 2, QBLK, PBLK), BF16),
            pltpu.VMEM((48, LANES, LANES), F32),
            pltpu.SemaphoreType.DMA((3,)),
            pltpu.SemaphoreType.DMA((6,)),
            pltpu.SemaphoreType.DMA((4,)),
        ]
        + [pltpu.VMEM(t.shape, t.dtype) for t in tables]
        + [pltpu.VMEM((LANES, 48, LANES), BF16)],
        compiler_params=pltpu.CompilerParams(vmem_limit_bytes=CONV_LIMIT),
        cost_estimate=pl.CostEstimate(flops=64 * 10**8, bytes_accessed=8 * 2**20, transcendentals=0),
        name="convolve",
    )(*(in_hbm(x) for x in (data, *tables))).reshape(LANES * 48, LANES)


def hidden_kernel(
    side_ref, scales_ref, split_ref, mix_mine, mix_theirs, conv_hbm, mine_hbm, theirs_hbm,
    hidden_ref, shuffled_ref, conv_ref, tokens_ref, mix_ref, wide, normed, sems, conv_sems,
):
    side = side_ref[0]
    width = hidden_ref.shape[2]
    count = hidden_ref.shape[1]
    start = pl.multiple_of(side * count, count)
    quarter = conv_hbm.shape[0] // 4
    arrivals = []
    for part in range(4):
        at = slice(part * quarter, (part + 1) * quarter)
        arrivals.append(pltpu.make_async_copy(conv_hbm.at[at], conv_ref.at[at], conv_sems.at[part]))
        arrivals[-1].start()
    copies = [
        pltpu.make_async_copy(mine_hbm.at[pl.ds(start, count)], tokens_ref.at[0], sems.at[0]),
        pltpu.make_async_copy(theirs_hbm, tokens_ref.at[1], sems.at[1]),
        pltpu.make_async_copy(mix_mine, mix_ref.at[0], sems.at[2]),
        pltpu.make_async_copy(mix_theirs, mix_ref.at[1], sems.at[3]),
    ]
    copies[0].start()
    copies[1].start()
    split = split_ref[...]
    for part in range(4):
        at = slice(part * quarter, (part + 1) * quarter)
        arrivals[part].wait()
        wide[:, at, :] = jnp.swapaxes(conv_ref[at].astype(F32), 0, 1)
    copies[2].start()
    copies[3].start()
    copies[0].wait()
    copies[1].wait()
    for block in range(count // LANES):
        low, half = block // 2, block % 2
        rows = slice(block * LANES, (block + 1) * LANES)
        total = 0.0
        for s in range(2):
            home = side if s == 0 else 1 - side
            pieces = []
            for slot in range(3):
                turned = jnp.concatenate(
                    [
                        wide[home * 24 + ((slot * 2 + e) * 2 + half) * 2 + low].T
                        for e in range(2)
                    ],
                    axis=1,
                ).astype(BF16)
                conv = jnp.dot(turned, split, preferred_element_type=F32)
                cols = slice(slot * 256, (slot + 1) * 256)
                values = tokens_ref[s, rows, cols].astype(F32)
                mixed = conv + scales_ref[s, 0:1, cols] * values
                hidden = values + mixed * jax.nn.sigmoid(values)
                hidden_ref[s, rows, cols] = hidden
                pieces.append(jnp.sum(hidden, axis=1, keepdims=True))
            total = total + (pieces[0] + pieces[1] + pieces[2])
        mean = total / (2 * width)
        first = hidden_ref[0, rows, :] - mean
        second = hidden_ref[1, rows, :] - mean
        square = jnp.sum(first * first, axis=1, keepdims=True) + jnp.sum(second * second, axis=1, keepdims=True)
        scale = lax.rsqrt(square / (2 * width) + 1e-05)
        normed[0, rows, :] = (first * scale * scales_ref[0, 1:2, :]).astype(BF16)
        normed[1, rows, :] = (second * scale * scales_ref[1, 1:2, :]).astype(BF16)
    for s in range(2):
        copies[2 + s].wait()
        shuffled_ref[s] = jnp.dot(normed[s], mix_ref[s], preferred_element_type=F32).astype(BF16)


def make_hidden(side, conv, mine, theirs, scales, mix):
    rows = theirs.shape[0]
    conv = conv.reshape(LANES, 48, LANES)
    return pl.pallas_call(
        hidden_kernel,
        in_specs=[pl.BlockSpec(memory_space=pltpu.SMEM)]
        + [pl.BlockSpec(memory_space=pltpu.VMEM)] * 2
        + [pl.BlockSpec(memory_space=pltpu.HBM)] * 5,
        out_shape=[
            jax.ShapeDtypeStruct((2, rows, 768), F32),
            jax.ShapeDtypeStruct((2, rows, 1024), BF16),
        ],
        scratch_shapes=[
            pltpu.VMEM(conv.shape, BF16),
            pltpu.VMEM((2, rows, 768), BF16),
            pltpu.VMEM((2, *mix[0].shape), BF16),
            pltpu.VMEM((48, LANES, LANES), F32),
            pltpu.VMEM((2, rows, 768), BF16),
            pltpu.SemaphoreType.DMA((4,)),
            pltpu.SemaphoreType.DMA((4,)),
        ],
        compiler_params=pltpu.CompilerParams(vmem_limit_bytes=SMALL_LIMIT),
        cost_estimate=pl.CostEstimate(flops=3 * 10**9, bytes_accessed=12 * 2**20, transcendentals=10**6),
        name="hidden",
    )(
        side,
        scales,
        pair_split(LANES),
        *(pltpu.with_memory_space_constraint(x, pltpu.HBM) for x in (*mix, conv, mine, theirs)),
    )


def gelu(x):
    slope = math.sqrt(2.0 / math.pi)
    half = 0.5 * x
    return half + half * jnp.tanh(x * (slope + (slope * 0.044715) * (x * x)))


def mlp_kernel(
    first_row, side_ref, hidden_ref, shuffled_ref, up_mine, up_theirs, down_mine, down_theirs, mix_mine, mix_theirs,
    keep_ref, send_ref, down_buf, gathered,
):
    side = side_ref[0]
    rows = slice(first_row, first_row + keep_ref.shape[0])
    for group, (up_ref, down_ref) in enumerate(((up_mine, down_mine), (up_theirs, down_theirs))):
        home = side if group == 0 else 1 - side
        ups, places_at = [], []
        for c in range(2):
            lanes = pl.multiple_of((2 * home + c) * 256, 256)
            places_at.append(lanes)
            total = 0.0
            for s in range(2):
                start = pl.multiple_of((side if s == 0 else 1 - side) * 192, 192)
                mixed = shuffled_ref[s, rows, pl.ds(lanes, 256)][:, :192]
                total = total + jnp.dot(mixed, up_ref[c, pl.ds(start, 192), :], preferred_element_type=F32)
            ups.append(total)
        for c in range(2):
            active = gelu(ups[c]).astype(BF16)
            down_buf[group, c] = jnp.dot(active, down_ref[c], preferred_element_type=F32).astype(BF16)
        for c in range(2):
            for s in range(2):
                start = pl.multiple_of((side if s == 0 else 1 - side) * LANES, LANES)
                gathered[s, :, pl.ds(places_at[c], 256)] = down_buf[group, c, :, pl.ds(start, 256)]
    for s, (ref, mix_ref) in enumerate(((keep_ref, mix_mine), (send_ref, mix_theirs))):
        outcome = jnp.dot(gathered[s], mix_ref[...], preferred_element_type=F32)
        ref[...] = (hidden_ref[s, rows, :] + outcome).astype(BF16)


def mlp(side, hidden, shuffled, ups, downs, mix, first_row, rows):
    return pl.pallas_call(
        functools.partial(mlp_kernel, first_row),
        in_specs=[pl.BlockSpec(memory_space=pltpu.SMEM)] + [pl.BlockSpec(memory_space=pltpu.VMEM)] * 8,
        out_shape=[jax.ShapeDtypeStruct((rows, 768), BF16)] * 2,
        scratch_shapes=[pltpu.VMEM((2, 2, rows, 384), BF16), pltpu.VMEM((2, rows, 1024), BF16)],
        compiler_params=pltpu.CompilerParams(vmem_limit_bytes=SMALL_LIMIT),
        cost_estimate=pl.CostEstimate(
            flops=rows * 14 * 10**6, bytes_accessed=14 * 2**20, transcendentals=rows * 6144
        ),
        name="mlp",
    )(side, hidden, shuffled, *ups, *downs, *mix)


def choose(place_ref, want, got, passed, target, sem, begin):
    for core, source in ((want, got), (1 - want, passed)):
        @pl.when(place_ref[1] == core)
        def _():
            copy = pltpu.make_async_copy(source, target, sem)
            copy.start() if begin else copy.wait()


def places(shape, axis, offset, piece):
    row = lax.broadcasted_iota(jnp.int32, shape, axis)
    group = sum((row >= c * piece).astype(jnp.int32) for c in range(1, NB))
    target = lax.broadcasted_iota(jnp.int32, shape, 1 - axis)
    return (target == row + group * (256 - piece) + offset).astype(F32).astype(BF16)


def rearrange(home, b, weight_in, weight_out, first_ref, last_ref):
    inner = weight_in.shape[0]
    piece = inner // NB
    picked = jnp.dot(weight_in, places((inner, NB * 256), 0, b * piece, piece), preferred_element_type=F32)
    first_ref[b * inner : (b + 1) * inner, :] = picked.astype(BF16)
    offset = b * piece + jnp.where(home == 0, 0, 256 - 2 * piece)
    picked = jnp.dot(places((NB * 256, inner), 1, offset, piece), weight_out, preferred_element_type=F32)
    last_ref[:, b * inner : (b + 1) * inner] = picked.astype(BF16)


def prepare_mine_kernel(place_ref, in_ref, out_ref, first_ref, last_ref):
    for b in range(in_ref.shape[0]):
        rearrange(place_ref[0], b, in_ref[b], out_ref[b], first_ref, last_ref)


def prepare_theirs_kernel(
    place_ref, up_got, up_passed, down_got, down_passed,
    first_ref, last_ref, up_theirs, down_theirs, up_ref, down_ref, sems,
):
    inner = up_ref.shape[1]
    picks = [(0, up_got, up_passed, up_ref, sems.at[0]), (1, down_got, down_passed, down_ref, sems.at[1])]
    for pick in picks:
        choose(place_ref, *pick, True)
    for pick in picks:
        choose(place_ref, *pick, False)
    stores = [
        pltpu.make_async_copy(up_ref.at[:, :, pl.ds(inner, up_ref.shape[2] - inner)], up_theirs, sems.at[2]),
        pltpu.make_async_copy(down_ref.at[:, pl.ds(inner, down_ref.shape[1] - inner)], down_theirs, sems.at[3]),
    ]
    for store in stores:
        store.start()
    for b in range(up_ref.shape[0]):
        rearrange(1 - place_ref[0], b, up_ref[b, :, :inner], down_ref[b, :inner, :], first_ref, last_ref)
    for store in stores:
        store.wait()


def prepare_shapes(blocks, inner):
    return [
        jax.ShapeDtypeStruct((blocks * inner, NB * 256), BF16),
        jax.ShapeDtypeStruct((NB * 256, blocks * inner), BF16),
    ]


def prepare_mine(place, mix_in, mix_out):
    return pl.pallas_call(
        prepare_mine_kernel,
        in_specs=[pl.BlockSpec(memory_space=pltpu.SMEM)] + [pl.BlockSpec(memory_space=pltpu.VMEM)] * 2,
        out_specs=[pl.BlockSpec(memory_space=pltpu.VMEM)] * 2,
        out_shape=prepare_shapes(mix_in.shape[0], mix_in.shape[1]),
        compiler_params=pltpu.CompilerParams(vmem_limit_bytes=SMALL_LIMIT),
        cost_estimate=pl.CostEstimate(flops=10**9, bytes_accessed=2**20, transcendentals=0),
        name="prepare_mine",
    )(place, mix_in, mix_out)


def prepare_theirs(place, ups, downs):
    blocks, inner, wide = ups[0].shape
    arrays = [*ups, *downs]
    return pl.pallas_call(
        prepare_theirs_kernel,
        in_specs=[pl.BlockSpec(memory_space=pltpu.SMEM)] + [pl.BlockSpec(memory_space=pltpu.HBM)] * 4,
        out_specs=[pl.BlockSpec(memory_space=pltpu.VMEM)] * 2 + [pl.BlockSpec(memory_space=pltpu.HBM)] * 2,
        out_shape=prepare_shapes(blocks, inner)
        + [pltpu.HBM((blocks, inner, wide - inner), BF16), pltpu.HBM((blocks, wide - inner, inner), BF16)],
        scratch_shapes=[
            pltpu.VMEM(ups[0].shape, BF16),
            pltpu.VMEM(downs[0].shape, BF16),
            pltpu.SemaphoreType.DMA((4,)),
        ],
        compiler_params=pltpu.CompilerParams(vmem_limit_bytes=VMEM_LIMIT),
        cost_estimate=pl.CostEstimate(flops=10**6, bytes_accessed=2**16, transcendentals=0),
        name="prepare_theirs",
    )(place, *(pltpu.with_memory_space_constraint(x, pltpu.HBM) for x in arrays))


def make_per_device(chunks):
    def per_device(tokens, spectrum, skip, gain, mix_in, w_up, w_down, mix_out):
        groups = lax.axis_size("seq")
        both = ("seq", "ch")
        side = lax.axis_index("ch")
        core = lax.axis_index("seq") % 2
        swap = [(0, 1), (1, 0)]
        step = groups // 2

        def near(which):
            return [
                (s * 2 + h, (s ^ step) * 2 + 1 - h) for h in range(2) for s in range(groups) if s % 2 == which
            ]

        def across(which):
            return [(s, s ^ 1) for s in range(groups) if s % 2 == which]

        count = tokens.shape[0] // 2
        place = jnp.stack([side, core]).astype(jnp.int32)
        packed = pack(tokens, spectrum)
        data = lax.all_to_all(packed, "seq", split_axis=0, concat_axis=0, tiled=True)

        weights = (jnp.concatenate([mix_in, w_up], axis=2), jnp.concatenate([mix_out, w_down], axis=1))
        got = [lax.ppermute(w, both, near(which)) for which, w in enumerate(weights)]
        theirs = lax.ppermute(lax.dynamic_slice_in_dim(tokens, (1 - side) * count, count, axis=0), "ch", swap)
        scales_mine = jnp.stack([skip, gain])
        scales = jnp.stack([scales_mine, lax.ppermute(scales_mine, "ch", swap)])
        first_mine, last_mine = prepare_mine(place, mix_in, mix_out)
        tables = [jnp.asarray(t) for t in make_tables(groups)]
        data, first_mine, last_mine, theirs, scales, tables = lax.optimization_barrier(
            (data, first_mine, last_mine, theirs, scales, tables)
        )
        conv = convolve(data, tables)

        _, got = lax.optimization_barrier((conv, got))
        conv = lax.all_to_all(conv, both, split_axis=0, concat_axis=0, tiled=True)
        passed = [lax.ppermute(g, "seq", across(which)) for which, g in enumerate(got)]
        first_theirs, last_theirs, up_theirs, down_theirs = prepare_theirs(
            place, (got[0], passed[0]), (got[1], passed[1])
        )
        mix_first = (first_mine, first_theirs)
        mix_last = (last_mine, last_theirs)
        hidden, shuffled = make_hidden(place, conv, tokens, theirs, scales, mix_first)
        out = jnp.zeros(tokens.shape, tokens.dtype)
        at = 0
        for rows in chunks:
            keep, send = mlp(place, hidden, shuffled, (w_up, up_theirs), (w_down, down_theirs), mix_last, at, rows)
            place, send = lax.optimization_barrier((place, send))
            sent = lax.ppermute(send, "ch", swap)
            out = lax.dynamic_update_slice_in_dim(out, keep, side * count + at, axis=0)
            out = lax.dynamic_update_slice_in_dim(out, sent, (1 - side) * count + at, axis=0)
            at += rows
        return out

    return per_device


def solution(mesh):
    return jax.shard_map(
        make_per_device((208, 240, 64)),
        mesh=mesh,
        in_specs=(
            P("seq", "ch"),
            P(None, "seq", None, "ch"),
            P("ch"),
            P("ch"),
            P("ch", None, None),
            P("ch", None, None),
            P("ch", None, None),
            P("ch", None, None),
        ),
        out_specs=P("seq", "ch"),
        check_vma=False,
    )
```

```python
import functools
import math

import jax
import jax.numpy as jnp
import ml_dtypes
import numpy as np
from jax import lax
from jax.experimental import pallas as pl
from jax.experimental.pallas import tpu as pltpu
from jax.sharding import PartitionSpec as P

D = 1536
NB = 4
PBLK = 256
QBLK = 512
LANES = 128
F32 = jnp.float32
BF16 = jnp.bfloat16
VMEM_LIMIT = 56 * 1024 * 1024
SMALL_LIMIT = 32 * 1024 * 1024
CONV_LIMIT = 40 * 1024 * 1024


def dft_numpy(length):
    index = np.arange(length, dtype=np.int64)
    angle = (index[:, None] * index[None, :] % length).astype(np.float32)
    angle = angle * np.float32(2.0 * math.pi / length)
    return (
        np.cos(angle).astype(ml_dtypes.bfloat16).astype(np.float32),
        np.sin(angle).astype(ml_dtypes.bfloat16).astype(np.float32),
    )


def make_tables(groups):
    low = QBLK // groups
    order = (np.arange(groups)[None, :] * low + np.arange(low)[:, None]).reshape(-1)
    cos_long, sin_long = dft_numpy(QBLK)
    cos_long, sin_long = cos_long[order][:, order], sin_long[order][:, order]
    cos_short, sin_short = dft_numpy(PBLK)
    second = np.block([[cos_short, -sin_short], [sin_short, cos_short]])
    third = np.block([[cos_short, sin_short], [-sin_short, cos_short]])
    seq_len = PBLK * QBLK
    angle = (order[:, None].astype(np.int64) * np.arange(PBLK)[None, :] % seq_len).astype(np.float32)
    angle = angle * np.float32(2.0 * math.pi / seq_len)
    half = [t.astype(ml_dtypes.bfloat16) for t in (cos_long, -sin_long, second, third)]
    return half + [np.cos(angle).astype(np.float32), np.sin(angle).astype(np.float32)]


def pair_split(pairs):
    table = np.zeros((2 * pairs, 2 * pairs), np.float32)
    for e in range(2):
        for d in range(pairs):
            table[e * pairs + d, 2 * d + e] = 1.0
    return table.astype(ml_dtypes.bfloat16)


def nt_dot(left, right):
    return lax.dot_general(left, right, (((1,), (1,)), ((), ())), preferred_element_type=F32)


def pack_kernel(tokens_ref, spectrum_ref, split_ref, out_ref, wide):
    split = split_ref[...]
    count = split.shape[0] // 2
    for low in range(4):
        turned = nt_dot(split, tokens_ref[low * 256 : (low + 1) * 256, :])
        for e in range(2):
            for half in range(2):
                wide[e * 8 + half * 4 + low] = turned[
                    e * count : (e + 1) * count, half * LANES : (half + 1) * LANES
                ]
    row = lax.broadcasted_iota(jnp.int32, (count, LANES), 0)
    pick = (row == lax.broadcasted_iota(jnp.int32, (count, LANES), 1)).astype(F32).astype(BF16)
    for part in range(2):
        for low in range(4):
            turned = spectrum_ref[part, low].astype(F32).T
            for half in range(2):
                wide[16 + part * 8 + half * 4 + low] = turned[:, half * LANES : (half + 1) * LANES]
    out_ref[...] = jnp.swapaxes(wide[...], 0, 1).astype(BF16)


def pack(tokens, spectrum):
    count = LANES
    return pl.pallas_call(
        pack_kernel,
        grid=(3,),
        in_specs=[
            pl.BlockSpec((1024, 2 * LANES), lambda i: (0, i)),
            pl.BlockSpec((2, 4, 256, LANES), lambda i: (0, 0, 0, i)),
            pl.BlockSpec((2 * LANES, 2 * LANES), lambda i: (0, 0)),
        ],
        out_specs=pl.BlockSpec((count, 32, LANES), lambda i: (0, i, 0)),
        out_shape=jax.ShapeDtypeStruct((LANES, 96, LANES), BF16),
        scratch_shapes=[pltpu.VMEM((32, count, LANES), F32)],
        compiler_params=pltpu.CompilerParams(vmem_limit_bytes=VMEM_LIMIT),
        cost_estimate=pl.CostEstimate(flops=2 * 10**9, bytes_accessed=6 * 2**20, transcendentals=0),
        name="pack",
    )(tokens, spectrum, pair_split(count))


def conv_kernel(data_hbm, *rest):
    sources, (out_hbm, data, wide, back, outs, sems, table_sems, out_sems), tables = rest[:6], rest[6:14], rest[14:]
    cos_long_ref, sin_long_ref, second_ref, third_ref, cos_ref, sin_ref, staged = tables

    def fetch(slot, part):
        at = pl.ds(part * 32, 32)
        return pltpu.make_async_copy(
            data_hbm.at[at, pl.ds(slot * 32, 32), :], data.at[slot, at], sems.at[slot * 4 + part]
        )

    loads = [pltpu.make_async_copy(sources[i], tables[i], table_sems.at[i]) for i in range(6)]
    for part in range(4):
        fetch(0, part).start()
    for i in (0, 1, 4, 5, 2, 3):
        loads[i].start()
    for slot in (1, 2):
        for part in range(4):
            fetch(slot, part).start()

    def filters(now, part):
        return jnp.concatenate(
            [
                jnp.concatenate([wide[now, 16 + part * 8 + half * 4 + low] for half in range(2)], axis=1)
                for low in range(4)
            ],
            axis=0,
        )

    for slot in range(3):
        now = slot % 2
        for part in range(4):
            at = slice(part * 32, (part + 1) * 32)
            fetch(slot, part).wait()
            wide[now, :, at, :] = jnp.swapaxes(data[slot, at].astype(F32), 0, 1)
        if slot == 0:
            loads[0].wait()
            loads[1].wait()
        channels = range(2)
        blocks = [
            jnp.concatenate(
                [
                    jnp.concatenate([wide[now, e * 8 + half * 4 + low] for half in range(2)], axis=1).astype(BF16)
                    for low in range(4)
                ],
                axis=0,
            )
            for e in channels
        ]
        first_real = [jnp.dot(cos_long_ref[...], block, preferred_element_type=F32) for block in blocks]
        first_imag = [jnp.dot(sin_long_ref[...], block, preferred_element_type=F32) for block in blocks]
        if slot == 0:
            for i in (4, 5, 2, 3):
                loads[i].wait()
        turn_cos, turn_sin = cos_ref[...], sin_ref[...]
        turned = [
            jnp.concatenate(
                [
                    (first_real[e] * turn_cos + first_imag[e] * turn_sin).astype(BF16),
                    (first_imag[e] * turn_cos - first_real[e] * turn_sin).astype(BF16),
                ],
                axis=1,
            )
            for e in channels
        ]
        spectral = [jnp.dot(turned[e], second_ref[...], preferred_element_type=F32) for e in channels]
        filter_real, filter_imag = filters(now, 0), filters(now, 1)
        filtered = [
            jnp.concatenate(
                [
                    (spectral[e][:, :PBLK] * filter_real - spectral[e][:, PBLK:] * filter_imag).astype(BF16),
                    (spectral[e][:, :PBLK] * filter_imag + spectral[e][:, PBLK:] * filter_real).astype(BF16),
                ],
                axis=1,
            )
            for e in channels
        ]
        third = [jnp.dot(filtered[e], third_ref[...], preferred_element_type=F32) for e in channels]
        for e in channels:
            back_real, back_imag = third[e][:, :PBLK], third[e][:, PBLK:]
            back[e, 0] = (back_real * turn_cos - back_imag * turn_sin).astype(BF16)
            back[e, 1] = (back_real * turn_sin + back_imag * turn_cos).astype(BF16)
        for e in channels:
            conv = jnp.dot(cos_long_ref[...], back[e, 0], preferred_element_type=F32)
            conv = conv + jnp.dot(sin_long_ref[...], back[e, 1], preferred_element_type=F32)
            conv = conv * (1.0 / (PBLK * QBLK))
            for low in range(4):
                for half in range(2):
                    row = (low // 2) * 24 + ((slot * 2 + e) * 2 + half) * 2 + low % 2
                    outs[row] = conv[low * LANES : (low + 1) * LANES, half * LANES : (half + 1) * LANES]

    stores = []
    for part in range(4):
        at = slice(part * 32, (part + 1) * 32)
        staged[at] = jnp.swapaxes(outs[:, at, :], 0, 1).astype(BF16)
        stores.append(pltpu.make_async_copy(staged.at[at], out_hbm.at[at], out_sems.at[part]))
        stores[-1].start()
    for store in stores:
        store.wait()


def convolve(data, tables):
    in_hbm = lambda x: pltpu.with_memory_space_constraint(x, pltpu.HBM)
    return pl.pallas_call(
        conv_kernel,
        in_specs=[pl.BlockSpec(memory_space=pltpu.HBM)] * (1 + len(tables)),
        out_specs=pl.BlockSpec(memory_space=pltpu.HBM),
        out_shape=pltpu.HBM((LANES, 48, LANES), BF16),
        scratch_shapes=[
            pltpu.VMEM((3, LANES, 32, LANES), BF16),
            pltpu.VMEM((2, 32, LANES, LANES), F32),
            pltpu.VMEM((2, 2, QBLK, PBLK), BF16),
            pltpu.VMEM((48, LANES, LANES), F32),
            pltpu.SemaphoreType.DMA((12,)),
            pltpu.SemaphoreType.DMA((6,)),
            pltpu.SemaphoreType.DMA((4,)),
        ]
        + [pltpu.VMEM(t.shape, t.dtype) for t in tables]
        + [pltpu.VMEM((LANES, 48, LANES), BF16)],
        compiler_params=pltpu.CompilerParams(vmem_limit_bytes=CONV_LIMIT),
        cost_estimate=pl.CostEstimate(flops=64 * 10**8, bytes_accessed=8 * 2**20, transcendentals=0),
        name="convolve",
    )(*(in_hbm(x) for x in (data, *tables))).reshape(LANES * 48, LANES)


def hidden_kernel(
    side_ref, scales_ref, split_ref, mix_mine, mix_theirs, conv_hbm, mine_hbm, theirs_hbm,
    hidden_ref, shuffled_ref, conv_ref, tokens_ref, mix_ref, wide, normed, sems, conv_sems,
):
    side = side_ref[0]
    width = hidden_ref.shape[2]
    count = hidden_ref.shape[1]
    start = pl.multiple_of(side * count, count)
    quarter = conv_hbm.shape[0] // 4
    arrivals = []
    for part in range(4):
        at = slice(part * quarter, (part + 1) * quarter)
        arrivals.append(pltpu.make_async_copy(conv_hbm.at[at], conv_ref.at[at], conv_sems.at[part]))
        arrivals[-1].start()
    copies = [
        pltpu.make_async_copy(mine_hbm.at[pl.ds(start, count)], tokens_ref.at[0], sems.at[0]),
        pltpu.make_async_copy(theirs_hbm, tokens_ref.at[1], sems.at[1]),
        pltpu.make_async_copy(mix_mine, mix_ref.at[0], sems.at[2]),
        pltpu.make_async_copy(mix_theirs, mix_ref.at[1], sems.at[3]),
    ]
    copies[0].start()
    copies[1].start()
    split = split_ref[...]
    for part in range(4):
        at = slice(part * quarter, (part + 1) * quarter)
        arrivals[part].wait()
        wide[:, at, :] = jnp.swapaxes(conv_ref[at].astype(F32), 0, 1)
    copies[2].start()
    copies[3].start()
    copies[0].wait()
    copies[1].wait()
    for block in range(count // LANES):
        low, half = block // 2, block % 2
        rows = slice(block * LANES, (block + 1) * LANES)
        total = 0.0
        for s in range(2):
            home = side if s == 0 else 1 - side
            pieces = []
            for slot in range(3):
                turned = jnp.concatenate(
                    [
                        wide[home * 24 + ((slot * 2 + e) * 2 + half) * 2 + low].T
                        for e in range(2)
                    ],
                    axis=1,
                ).astype(BF16)
                conv = jnp.dot(turned, split, preferred_element_type=F32)
                cols = slice(slot * 256, (slot + 1) * 256)
                values = tokens_ref[s, rows, cols].astype(F32)
                mixed = conv + scales_ref[s, 0:1, cols] * values
                hidden = values + mixed * jax.nn.sigmoid(values)
                hidden_ref[s, rows, cols] = hidden
                pieces.append(jnp.sum(hidden, axis=1, keepdims=True))
            total = total + (pieces[0] + pieces[1] + pieces[2])
        mean = total / (2 * width)
        first = hidden_ref[0, rows, :] - mean
        second = hidden_ref[1, rows, :] - mean
        square = jnp.sum(first * first, axis=1, keepdims=True) + jnp.sum(second * second, axis=1, keepdims=True)
        scale = lax.rsqrt(square / (2 * width) + 1e-05)
        normed[0, rows, :] = (first * scale * scales_ref[0, 1:2, :]).astype(BF16)
        normed[1, rows, :] = (second * scale * scales_ref[1, 1:2, :]).astype(BF16)
    for s in range(2):
        copies[2 + s].wait()
        shuffled_ref[s] = jnp.dot(normed[s], mix_ref[s], preferred_element_type=F32).astype(BF16)


def make_hidden(side, conv, mine, theirs, scales, mix):
    rows = theirs.shape[0]
    conv = conv.reshape(LANES, 48, LANES)
    return pl.pallas_call(
        hidden_kernel,
        in_specs=[pl.BlockSpec(memory_space=pltpu.SMEM)]
        + [pl.BlockSpec(memory_space=pltpu.VMEM)] * 2
        + [pl.BlockSpec(memory_space=pltpu.HBM)] * 5,
        out_shape=[
            jax.ShapeDtypeStruct((2, rows, 768), F32),
            jax.ShapeDtypeStruct((2, rows, 1024), BF16),
        ],
        scratch_shapes=[
            pltpu.VMEM(conv.shape, BF16),
            pltpu.VMEM((2, rows, 768), BF16),
            pltpu.VMEM((2, *mix[0].shape), BF16),
            pltpu.VMEM((48, LANES, LANES), F32),
            pltpu.VMEM((2, rows, 768), BF16),
            pltpu.SemaphoreType.DMA((4,)),
            pltpu.SemaphoreType.DMA((4,)),
        ],
        compiler_params=pltpu.CompilerParams(vmem_limit_bytes=SMALL_LIMIT),
        cost_estimate=pl.CostEstimate(flops=3 * 10**9, bytes_accessed=12 * 2**20, transcendentals=10**6),
        name="hidden",
    )(
        side,
        scales,
        pair_split(LANES),
        *(pltpu.with_memory_space_constraint(x, pltpu.HBM) for x in (*mix, conv, mine, theirs)),
    )


def gelu(x):
    slope = math.sqrt(2.0 / math.pi)
    half = 0.5 * x
    return half + half * jnp.tanh(x * (slope + (slope * 0.044715) * (x * x)))


def mlp_kernel(
    first_row, side_ref, hidden_ref, shuffled_ref, up_mine, up_theirs, down_mine, down_theirs, mix_mine, mix_theirs,
    keep_ref, send_ref, down_buf, gathered,
):
    side = side_ref[0]
    rows = slice(first_row, first_row + keep_ref.shape[0])
    for group, (up_ref, down_ref) in enumerate(((up_mine, down_mine), (up_theirs, down_theirs))):
        home = side if group == 0 else 1 - side
        ups, places_at = [], []
        for c in range(2):
            lanes = pl.multiple_of((2 * home + c) * 256, 256)
            places_at.append(lanes)
            total = 0.0
            for s in range(2):
                start = pl.multiple_of((side if s == 0 else 1 - side) * 192, 192)
                mixed = shuffled_ref[s, rows, pl.ds(lanes, 256)][:, :192]
                total = total + jnp.dot(mixed, up_ref[c, pl.ds(start, 192), :], preferred_element_type=F32)
            ups.append(total)
        for c in range(2):
            active = gelu(ups[c]).astype(BF16)
            down_buf[group, c] = jnp.dot(active, down_ref[c], preferred_element_type=F32).astype(BF16)
        for c in range(2):
            for s in range(2):
                start = pl.multiple_of((side if s == 0 else 1 - side) * LANES, LANES)
                gathered[s, :, pl.ds(places_at[c], 256)] = down_buf[group, c, :, pl.ds(start, 256)]
    for s, (ref, mix_ref) in enumerate(((keep_ref, mix_mine), (send_ref, mix_theirs))):
        outcome = jnp.dot(gathered[s], mix_ref[...], preferred_element_type=F32)
        ref[...] = (hidden_ref[s, rows, :] + outcome).astype(BF16)


def mlp(side, hidden, shuffled, ups, downs, mix, first_row, rows):
    return pl.pallas_call(
        functools.partial(mlp_kernel, first_row),
        in_specs=[pl.BlockSpec(memory_space=pltpu.SMEM)] + [pl.BlockSpec(memory_space=pltpu.VMEM)] * 8,
        out_shape=[jax.ShapeDtypeStruct((rows, 768), BF16)] * 2,
        scratch_shapes=[pltpu.VMEM((2, 2, rows, 384), BF16), pltpu.VMEM((2, rows, 1024), BF16)],
        compiler_params=pltpu.CompilerParams(vmem_limit_bytes=SMALL_LIMIT),
        cost_estimate=pl.CostEstimate(
            flops=rows * 14 * 10**6, bytes_accessed=14 * 2**20, transcendentals=rows * 6144
        ),
        name="mlp",
    )(side, hidden, shuffled, *ups, *downs, *mix)


def choose(place_ref, want, got, passed, target, sem, begin):
    for core, source in ((want, got), (1 - want, passed)):
        @pl.when(place_ref[1] == core)
        def _():
            copy = pltpu.make_async_copy(source, target, sem)
            copy.start() if begin else copy.wait()


def places(shape, axis, offset, piece):
    row = lax.broadcasted_iota(jnp.int32, shape, axis)
    group = sum((row >= c * piece).astype(jnp.int32) for c in range(1, NB))
    target = lax.broadcasted_iota(jnp.int32, shape, 1 - axis)
    return (target == row + group * (256 - piece) + offset).astype(F32).astype(BF16)


def rearrange(home, b, weight_in, weight_out, first_ref, last_ref):
    inner = weight_in.shape[0]
    piece = inner // NB
    picked = jnp.dot(weight_in, places((inner, NB * 256), 0, b * piece, piece), preferred_element_type=F32)
    first_ref[b * inner : (b + 1) * inner, :] = picked.astype(BF16)
    offset = b * piece + jnp.where(home == 0, 0, 256 - 2 * piece)
    picked = jnp.dot(places((NB * 256, inner), 1, offset, piece), weight_out, preferred_element_type=F32)
    last_ref[:, b * inner : (b + 1) * inner] = picked.astype(BF16)


def prepare_mine_kernel(place_ref, in_ref, out_ref, first_ref, last_ref):
    for b in range(in_ref.shape[0]):
        rearrange(place_ref[0], b, in_ref[b], out_ref[b], first_ref, last_ref)


def prepare_theirs_kernel(
    place_ref, up_got, up_passed, down_got, down_passed,
    first_ref, last_ref, up_theirs, down_theirs, up_ref, down_ref, sems,
):
    inner = up_ref.shape[1]
    picks = [(0, up_got, up_passed, up_ref, sems.at[0]), (1, down_got, down_passed, down_ref, sems.at[1])]
    for pick in picks:
        choose(place_ref, *pick, True)
    for pick in picks:
        choose(place_ref, *pick, False)
    stores = [
        pltpu.make_async_copy(up_ref.at[:, :, pl.ds(inner, up_ref.shape[2] - inner)], up_theirs, sems.at[2]),
        pltpu.make_async_copy(down_ref.at[:, pl.ds(inner, down_ref.shape[1] - inner)], down_theirs, sems.at[3]),
    ]
    for store in stores:
        store.start()
    for b in range(up_ref.shape[0]):
        rearrange(1 - place_ref[0], b, up_ref[b, :, :inner], down_ref[b, :inner, :], first_ref, last_ref)
    for store in stores:
        store.wait()


def prepare_shapes(blocks, inner):
    return [
        jax.ShapeDtypeStruct((blocks * inner, NB * 256), BF16),
        jax.ShapeDtypeStruct((NB * 256, blocks * inner), BF16),
    ]


def prepare_mine(place, mix_in, mix_out):
    return pl.pallas_call(
        prepare_mine_kernel,
        in_specs=[pl.BlockSpec(memory_space=pltpu.SMEM)] + [pl.BlockSpec(memory_space=pltpu.VMEM)] * 2,
        out_specs=[pl.BlockSpec(memory_space=pltpu.VMEM)] * 2,
        out_shape=prepare_shapes(mix_in.shape[0], mix_in.shape[1]),
        compiler_params=pltpu.CompilerParams(vmem_limit_bytes=SMALL_LIMIT),
        cost_estimate=pl.CostEstimate(flops=10**9, bytes_accessed=2**20, transcendentals=0),
        name="prepare_mine",
    )(place, mix_in, mix_out)


def prepare_theirs(place, ups, downs):
    blocks, inner, wide = ups[0].shape
    arrays = [*ups, *downs]
    return pl.pallas_call(
        prepare_theirs_kernel,
        in_specs=[pl.BlockSpec(memory_space=pltpu.SMEM)] + [pl.BlockSpec(memory_space=pltpu.HBM)] * 4,
        out_specs=[pl.BlockSpec(memory_space=pltpu.VMEM)] * 2 + [pl.BlockSpec(memory_space=pltpu.HBM)] * 2,
        out_shape=prepare_shapes(blocks, inner)
        + [pltpu.HBM((blocks, inner, wide - inner), BF16), pltpu.HBM((blocks, wide - inner, inner), BF16)],
        scratch_shapes=[
            pltpu.VMEM(ups[0].shape, BF16),
            pltpu.VMEM(downs[0].shape, BF16),
            pltpu.SemaphoreType.DMA((4,)),
        ],
        compiler_params=pltpu.CompilerParams(vmem_limit_bytes=VMEM_LIMIT),
        cost_estimate=pl.CostEstimate(flops=10**6, bytes_accessed=2**16, transcendentals=0),
        name="prepare_theirs",
    )(place, *(pltpu.with_memory_space_constraint(x, pltpu.HBM) for x in arrays))


def make_per_device(chunks):
    def per_device(tokens, spectrum, skip, gain, mix_in, w_up, w_down, mix_out):
        groups = lax.axis_size("seq")
        both = ("seq", "ch")
        side = lax.axis_index("ch")
        core = lax.axis_index("seq") % 2
        swap = [(0, 1), (1, 0)]
        step = groups // 2

        def near(which):
            return [
                (s * 2 + h, (s ^ step) * 2 + 1 - h) for h in range(2) for s in range(groups) if s % 2 == which
            ]

        def across(which):
            return [(s, s ^ 1) for s in range(groups) if s % 2 == which]

        count = tokens.shape[0] // 2
        place = jnp.stack([side, core]).astype(jnp.int32)
        packed = pack(tokens, spectrum)
        data = lax.all_to_all(packed, "seq", split_axis=0, concat_axis=0, tiled=True)

        weights = (jnp.concatenate([mix_in, w_up], axis=2), jnp.concatenate([mix_out, w_down], axis=1))
        got = [lax.ppermute(w, both, near(which)) for which, w in enumerate(weights)]
        theirs = lax.ppermute(lax.dynamic_slice_in_dim(tokens, (1 - side) * count, count, axis=0), "ch", swap)
        scales_mine = jnp.stack([skip, gain])
        scales = jnp.stack([scales_mine, lax.ppermute(scales_mine, "ch", swap)])
        first_mine, last_mine = prepare_mine(place, mix_in, mix_out)
        tables = [jnp.asarray(t) for t in make_tables(groups)]
        data, first_mine, last_mine, theirs, scales, tables = lax.optimization_barrier(
            (data, first_mine, last_mine, theirs, scales, tables)
        )
        conv = convolve(data, tables)

        _, got = lax.optimization_barrier((conv, got))
        conv = lax.all_to_all(conv, both, split_axis=0, concat_axis=0, tiled=True)
        passed = [lax.ppermute(g, "seq", across(which)) for which, g in enumerate(got)]
        first_theirs, last_theirs, up_theirs, down_theirs = prepare_theirs(
            place, (got[0], passed[0]), (got[1], passed[1])
        )
        mix_first = (first_mine, first_theirs)
        mix_last = (last_mine, last_theirs)
        hidden, shuffled = make_hidden(place, conv, tokens, theirs, scales, mix_first)
        out = jnp.zeros(tokens.shape, tokens.dtype)
        at = 0
        for rows in chunks:
            keep, send = mlp(place, hidden, shuffled, (w_up, up_theirs), (w_down, down_theirs), mix_last, at, rows)
            place, send = lax.optimization_barrier((place, send))
            sent = lax.ppermute(send, "ch", swap)
            out = lax.dynamic_update_slice_in_dim(out, keep, side * count + at, axis=0)
            out = lax.dynamic_update_slice_in_dim(out, sent, (1 - side) * count + at, axis=0)
            at += rows
        return out

    return per_device


def solution(mesh):
    return jax.shard_map(
        make_per_device((160, 192, 112, 48)),
        mesh=mesh,
        in_specs=(
            P("seq", "ch"),
            P(None, "seq", None, "ch"),
            P("ch"),
            P("ch"),
            P("ch", None, None),
            P("ch", None, None),
            P("ch", None, None),
            P("ch", None, None),
        ),
        out_specs=P("seq", "ch"),
        check_vma=False,
    )
```
